512 devices in a mesh: pool: 64 (over z, x), tp: 8 (over y, core).
Axes of the slice: x: 4, y: 4, z: 16, core: 2. Of those that a mesh axis runs over, the one named last changes fastest.
Arguments:
- queries: bfloat16 [128, 8192], P('pool', 'tp'), may hold values from -12 to 12
- key_cache: bfloat16 [8, 1024, 512, 128], P('tp', 'pool'), may hold values from -12 to 12
- value_cache: bfloat16 [8, 1024, 512, 128], P('tp', 'pool'), may hold values from -8 to 8
- out_weight: bfloat16 [8192, 8192], P('tp', 'pool'), may hold values from -0.0625 to 0.0625
- lengths: int32 [128], replicated, may hold values from 1 to 16384
- block_table: int32 [128, 32], replicated, may hold values from -1 to 1023, as said below
Outputs:
- output: bfloat16 [128, 8192], P('tp', 'pool')
The draws below stay inside these ranges and needn't reach their ends.
Inputs may be any that keep to these rules, and one draw needn't show every extreme that they name: `block_table`: entries of one row's table past its ceil(length / 512) blocks are -1, the others are distinct global slot ids, and each slot belongs to at most one row; slot s lies on index floor(s / 16) of pool.
All inputs are finite; a program needn't handle non-finite values.
Results may differ from the reference program's by a relative error of at most 0.0052.
Values may be sent and summed in bfloat16 or wider, within the bound.
A program may use at most 64 MiB of HBM per device.

```python
import math
import jax
import jax.numpy as jnp
from jax import lax

HEADS = 64
KVH = 8
HD = 128
D = 8192
BLK = 512
MAXB = 32
ROWS = 128
SLOTS_ALL = 1024


def layout(key):
    key = jax.random.fold_in(key, 11)
    row_index = jnp.arange(ROWS, dtype=jnp.int32)
    stepped = row_index * 1024 // max(ROWS - 1, 1)
    square = stepped * stepped // 1024
    cubed = square * stepped // 1024
    counts = 1 + (MAXB - 1) * cubed * cubed // (1024 * 1024)
    last_fill = jax.random.randint(jax.random.fold_in(key, 1), (ROWS,), 1, BLK + 1)
    last_fill = jnp.where(row_index == ROWS - 1, BLK, last_fill)
    sched_len = (counts - 1) * BLK + last_fill
    shuffle = jax.random.permutation(jax.random.fold_in(key, 2), ROWS)
    row_counts = counts[shuffle]
    row_lengths = sched_len[shuffle]
    starts = jnp.cumsum(row_counts) - row_counts
    slot_order = jax.random.permutation(jax.random.fold_in(key, 3), SLOTS_ALL).astype(jnp.int32)
    top_place = jnp.argmax(slot_order)
    slot_order = slot_order.at[top_place].set(slot_order[0]).at[0].set(SLOTS_ALL - 1)
    columns = jnp.arange(MAXB, dtype=jnp.int32)
    chosen_slots = slot_order[jnp.minimum(starts[:, None] + columns[None, :], SLOTS_ALL - 1)]
    table_rows = jnp.where(columns[None, :] < row_counts[:, None], chosen_slots, -1)
    return (row_lengths.astype(jnp.int32), table_rows.astype(jnp.int32))


def draw_lengths(key, part):
    return layout(key)[0]


def draw_block_table(key, part):
    return layout(key)[1]


def draw_queries(key, part):
    key = jax.random.fold_in(key, 5)
    key_one = jax.random.fold_in(key, 1)
    values = 2.0 * jax.random.normal(key_one, (ROWS, HEADS, HD), jnp.float32)
    return jnp.clip(values, -12.0, 12.0).reshape(ROWS, HEADS * HD).astype(jnp.bfloat16)


def draw_key_cache(key, part):
    key = jax.random.fold_in(key, 7)
    key_one = jax.random.fold_in(key, 1)
    values = jax.random.normal(key_one, (KVH, SLOTS_ALL, BLK, HD), jnp.float32)
    return jnp.clip(values, -12.0, 12.0).astype(jnp.bfloat16)


def block_scale(stream_key, dims, shards, low, high):
    def one(axis_at, parts):
        draws = jax.random.uniform(jax.random.fold_in(jax.random.fold_in(stream_key, 6), axis_at), (parts,), jnp.float32, low / len(shards), high / len(shards))
        return jnp.repeat(jnp.exp(draws), dims[axis_at] // parts).reshape((-1,) + (1,) * (len(dims) - axis_at - 1))

    gain = one(*shards[0])
    for cut in shards[1:]:
        gain = gain * one(*cut)
    return gain


def scatter_about(stream_key, shape, spread, bound, split=(), kind=jnp.bfloat16):
    drawn = spread * jax.random.normal(stream_key, shape, jnp.float32)
    if split:
        drawn = drawn * block_scale(stream_key, shape, split, -0.22, 0.18)
    return jnp.clip(drawn, -bound, bound).astype(kind)


def setup_inputs(seed: int = 0) -> dict:
    seeds = jax.random.split(jax.random.key(seed), 7)
    return {
        "queries": draw_queries(jax.random.fold_in(seeds[6], 71), 0),
        "key_cache": draw_key_cache(jax.random.fold_in(seeds[6], 71), 0),
        "value_cache": scatter_about(seeds[2], (KVH, SLOTS_ALL, BLK, HD), 2.0, 8.0, ((0, 8), (1, 64))),
        "out_weight": scatter_about(seeds[3], (HEADS * HD, D), (HEADS * HD) ** -0.5, 0.0625, ((0, 8), (1, 64))),
        "lengths": draw_lengths(jax.random.fold_in(seeds[6], 71), 0),
        "block_table": draw_block_table(jax.random.fold_in(seeds[6], 71), 0),
    }


FLOOR = -1e+30

def reference(queries, key_cache, value_cache, out_weight, lengths, block_table):
    group_size = HEADS // KVH
    scaling = 1.0 / math.sqrt(HD)
    offsets = jnp.arange(BLK, dtype=jnp.int32)

    def one_row(inputs):
        query_row, length_row, table_row = inputs
        grouped = query_row.astype(jnp.float32).reshape(KVH, group_size, HD)

        def one_block(running, block_idx):
            slot_id = table_row[block_idx]
            usable_block = slot_id >= 0
            slot_at = jnp.maximum(slot_id, 0).astype(jnp.int32)
            key_rows = lax.dynamic_index_in_dim(key_cache, slot_at, 1, keepdims=False).astype(jnp.float32)
            value_rows = lax.dynamic_index_in_dim(value_cache, slot_at, 1, keepdims=False).astype(jnp.float32)
            scores = jnp.einsum('kgd,ktd->kgt', grouped, key_rows) * scaling
            usable = (block_idx * BLK + offsets < length_row) & usable_block
            scores = jnp.where(usable[None, None, :], scores, FLOOR)
            block_max = lax.optimization_barrier(jnp.max(scores, axis=-1))
            weights = jnp.where(usable[None, None, :], jnp.exp(scores - block_max[..., None]), 0.0)
            block_sum = lax.optimization_barrier(jnp.sum(weights, axis=-1))
            rounded = lax.optimization_barrier(weights.astype(jnp.bfloat16)).astype(jnp.float32)
            block_out = jnp.einsum('kgt,ktd->kgd', rounded, value_rows)
            highest, denominator, numerator = running
            raised = jnp.maximum(highest, block_max)
            old_scale = jnp.exp(highest - raised)
            new_scale = jnp.exp(block_max - raised)
            return ((raised, denominator * old_scale + block_sum * new_scale, numerator * old_scale[..., None] + block_out * new_scale[..., None]), None)
        initial = (jnp.full((KVH, group_size), FLOOR, jnp.float32), jnp.zeros((KVH, group_size), jnp.float32), jnp.zeros((KVH, group_size, HD), jnp.float32))
        (highest, denominator, numerator), ignored = lax.scan(one_block, initial, jnp.arange(MAXB, dtype=jnp.int32))
        return (numerator / denominator[..., None]).reshape(HEADS * HD).astype(jnp.bfloat16)
    attended = lax.map(one_row, (queries, lengths, block_table))
    return jnp.dot(attended, out_weight, preferred_element_type=jnp.float32).astype(jnp.bfloat16)
```

```python
import functools
import math

import jax
import jax.numpy as jnp
from jax import lax
from jax.experimental import pallas as pl
from jax.experimental.pallas import tpu as pltpu
from jax.sharding import PartitionSpec as P

MESH = pl.DeviceIdType.MESH
FLOOR = -1e30
F32 = jnp.float32
BF16 = jnp.bfloat16

NZ, NX, NT = 16, 4, 8
ROWS, SLOTS, BLK, HD, GROUP, MAXB = 128, 16, 512, 128, 8, 32
PAIR = GROUP // NX
BAND = ROWS // NT
NEAR = 4
ZORDER = [(k - NEAR) % NZ for k in range(NZ)]
NEAR_N = 2 * NEAR + 1
FAR_FIRST = [8, 7, 9, 6, 10, 5, 11, 4, 12, 3, 13, 2, 14, 1, 15]


def dot(a, b, dims=((1,), (0,))):
    return lax.dot_general(a, b, (dims, ((), ())), preferred_element_type=F32)


def kernel(
    q_hbm,
    k_hbm,
    v_hbm,
    w_hbm,
    len_hbm,
    tab_hbm,
    out_ref,
    tab,
    lens,
    keys,
    vals,
    qall,
    sel,
    lims,
    hold,
    prob,
    o_f,
    stat_f,
    o_send,
    st_x,
    o_x,
    zst_send,
    zst,
    scale_t,
    zw,
    part,
    rs,
    att,
    wx,
    pl_send,
    pl_recv,
    loc_sem,
    sq,
    rq,
    sqx,
    rqx,
    sw,
    rw,
    sst,
    rst,
    so,
    ro,
    szs,
    rzs,
    srs,
    rrs,
    sag,
    rag,
    spl,
    rpl,
):
    pool = lax.axis_index("pool")
    t = lax.axis_index("tp")
    z = pool // NX
    x = pool % NX

    def at(dz, dx, dt):
        return {
            "pool": ((z + dz) % NZ) * NX + (x + dx) % NX,
            "tp": (t + dt) % NT,
        }

    def remote(src, dst, send, recv, to):
        copy = pltpu.make_async_remote_copy(
            src_ref=src,
            dst_ref=dst,
            send_sem=send,
            recv_sem=recv,
            device_id=to,
            device_id_type=MESH,
        )
        copy.start()
        return copy

    sends = []

    own = NEAR
    c_tab = pltpu.make_async_copy(tab_hbm, tab, loc_sem.at[0])
    c_len = pltpu.make_async_copy(len_hbm, lens, loc_sem.at[1])
    c_q = pltpu.make_async_copy(q_hbm, qall.at[0, own], loc_sem.at[2])
    c_k = pltpu.make_async_copy(k_hbm.at[0], keys, loc_sem.at[3])
    c_v = pltpu.make_async_copy(v_hbm.at[0], vals, loc_sem.at[4])
    c_w = pltpu.make_async_copy(
        w_hbm.at[pl.ds(pl.multiple_of(x * PAIR * HD, PAIR * HD), PAIR * HD)],
        wx.at[0],
        loc_sem.at[5],
    )
    plane = [(dx, dt) for dx in range(NX) for dt in range(NT) if (dx, dt) != (0, 0)]
    barrier = pltpu.get_barrier_semaphore()
    for dz in FAR_FIRST:
        pl.semaphore_signal(barrier, inc=1, device_id=at(dz, 0, 0), device_id_type=MESH)
    for dx, dt in plane:
        pl.semaphore_signal(barrier, inc=1, device_id=at(0, dx, dt), device_id_type=MESH)
    c_q.start()
    c_tab.start()
    c_len.start()
    c_k.start()
    c_v.start()
    c_w.start()

    c_tab.wait()
    c_len.wait()
    tab_t = tab[...].astype(F32)
    len_row = lens[...].astype(F32)
    sub = lax.broadcasted_iota(jnp.int32, (ROWS, ROWS), 0)
    lane = lax.broadcasted_iota(jnp.int32, (ROWS, ROWS), 1)
    sid = (pool * SLOTS + sub // GROUP).astype(F32)
    left = jnp.zeros((ROWS, ROWS), F32)
    sub4 = lax.broadcasted_iota(jnp.int32, (NX * SLOTS, ROWS), 0)
    sid4 = ((z * NX + (x + sub4 // SLOTS) % NX) * SLOTS + sub4 % SLOTS).astype(F32)
    held = jnp.zeros((NX * SLOTS, ROWS), F32)
    for b in range(MAXB):
        entry = tab_t[b : b + 1, :]
        left = jnp.where(entry == sid, len_row - float(BLK * b), left)
        held = jnp.where(entry == sid4, 1.0, held)
    hold[...] = held
    lims[...] = jnp.broadcast_to(jnp.sum(left, axis=1, keepdims=True), (ROWS, ROWS))
    row_of = jnp.sum(
        jnp.where(left > 0.0, (lane + 1).astype(F32), 0.0), axis=1, keepdims=True
    )
    key_col = (row_of - 1.0) * float(GROUP) + (sub[:, 0:1] % GROUP).astype(F32)
    j = lax.broadcasted_iota(jnp.int32, (1, ROWS * GROUP), 1)
    piece = j // 16
    dx_j = piece // NZ
    dz_j = piece % NZ - NEAR + NZ
    p_j = ((z + dz_j) % NZ) * NX + (x + dx_j) % NX
    key_row = ((2 * p_j + j % 2) * GROUP + (j % 16) // 2).astype(F32)
    for c in range(8):
        cut = slice(c * 128, (c + 1) * 128)
        sel[:, cut] = jnp.where(key_col == key_row[:, cut], 1.0, 0.0).astype(BF16)
    c_q.wait()
    pl.semaphore_wait(barrier, len(FAR_FIRST) + len(plane))

    place = {dz: k for k, dz in enumerate(ZORDER)}
    got = {}
    for dz in FAR_FIRST:
        k = place[(NZ - dz) % NZ]
        got[k] = remote(
            qall.at[0, own], qall.at[0, k], sq.at[dz], rq.at[k], at(dz, 0, 0)
        )
        sends.append(got[k])
    xgot = []
    for lo, hi, s in ((0, NEAR_N, 0), (NEAR_N, NZ, 1)):
        for k in range(lo, hi):
            if k != own:
                got[k].wait_recv()
        for dx in (2, 1, 3):
            e = (NX - dx) % NX
            copy = remote(
                qall.at[0, pl.ds(lo, hi - lo)],
                qall.at[e, pl.ds(lo, hi - lo)],
                sqx.at[dx, s],
                rqx.at[e, s],
                at(0, dx, 0),
            )
            xgot.append(copy)
            sends.append(copy)
    wgot = []
    for dx in (2, 1, 3):
        e = (NX - dx) % NX
        rows = pl.ds(pl.multiple_of(((x + dx) % NX) * PAIR * HD, PAIR * HD), PAIR * HD)
        copy = remote(w_hbm.at[rows], wx.at[e], sw.at[dx], rw.at[e], at(0, dx, 0))
        wgot.append(copy)
        sends.append(copy)
    c_k.wait()
    for copy in xgot:
        copy.wait_recv()

    picked = dot(sel[...], qall[...].reshape(ROWS * GROUP, HD))
    scaling = 1.0 / math.sqrt(HD)
    place_in = lax.broadcasted_iota(jnp.int32, (GROUP, BLK), 1).astype(F32)
    lane8 = lax.broadcasted_iota(jnp.int32, (GROUP, HD), 1)
    for s in range(SLOTS):
        mine = slice(GROUP * s, GROUP * (s + 1))
        scores = dot(picked[mine].astype(BF16), keys[s], ((1,), (1,))) * scaling
        usable = place_in < lims[mine, 0:1]
        scores = jnp.where(usable, scores, FLOOR)
        peak = jnp.max(scores, axis=1, keepdims=True)
        weights = jnp.where(usable, jnp.exp(scores - peak), 0.0)
        total = jnp.sum(weights, axis=1, keepdims=True)
        prob[s] = weights.astype(BF16)
        stat_f[pl.ds(s, GROUP, stride=SLOTS), :] = jnp.where(lane8 == 0, peak, total)
    mine_x = pl.ds(pl.multiple_of(x * PAIR * SLOTS, PAIR * SLOTS), PAIR * SLOTS)
    stgot = []
    for dx in (2, 1, 3):
        e = (NX - dx) % NX
        rows = pl.ds(pl.multiple_of(((x + dx) % NX) * PAIR * SLOTS, PAIR * SLOTS), PAIR * SLOTS)
        copy = remote(stat_f.at[rows], st_x.at[e], sst.at[dx], rst.at[e], at(0, dx, 0))
        stgot.append(copy)
        sends.append(copy)
    st_x[0] = stat_f[mine_x, :]
    c_v.wait()
    for s in range(SLOTS):
        o_f[pl.ds(s, GROUP, stride=SLOTS), :] = dot(prob[s], vals[s])
    o_send[...] = o_f[...].astype(BF16)
    ogot = []
    for dx in (2, 1, 3):
        e = (NX - dx) % NX
        rows = pl.ds(pl.multiple_of(((x + dx) % NX) * PAIR * SLOTS, PAIR * SLOTS), PAIR * SLOTS)
        copy = remote(o_send.at[rows], o_x.at[e], so.at[dx], ro.at[e], at(0, dx, 0))
        ogot.append(copy)
        sends.append(copy)
    o_x[0] = o_send[mine_x, :]

    for copy in stgot:
        copy.wait_recv()
    ws = []
    is_held = hold[...] > 0.0
    for hh in range(PAIR):
        cut = slice(hh * SLOTS, (hh + 1) * SLOTS)
        peak = jnp.concatenate([st_x[e, cut, 0:1] for e in range(NX)], axis=0)
        total = jnp.concatenate([st_x[e, cut, 1:2] for e in range(NX)], axis=0)
        top = jnp.max(jnp.where(is_held, peak, FLOOR), axis=0, keepdims=True)
        w = jnp.where(is_held, jnp.exp(peak - top), 0.0)
        ws.append(w.astype(BF16))
        zst_send[hh : hh + 1, :] = top
        zst_send[PAIR + hh : PAIR + hh + 1, :] = jnp.sum(w * total, axis=0, keepdims=True)
    zgot = []
    for dz in FAR_FIRST:
        e = NZ - dz
        copy = remote(zst_send, zst.at[e], szs.at[dz], rzs.at[e], at(dz, 0, 0))
        zgot.append(copy)
        sends.append(copy)
    zst[0] = zst_send[...]

    for copy in ogot:
        copy.wait_recv()
    for hh in range(PAIR):
        data = jnp.concatenate(
            [o_x[e, hh * SLOTS : (hh + 1) * SLOTS, :] for e in range(NX)], axis=0
        )
        part[:, hh * HD : (hh + 1) * HD] = dot(ws[hh], data, ((0,), (0,))).astype(BF16)
    rgot = []
    for dz in FAR_FIRST:
        e = NZ - dz
        band = ((z + dz) % NZ) % NT
        rows = pl.ds(pl.multiple_of(band * BAND, BAND), BAND)
        copy = remote(part.at[rows], rs.at[e], srs.at[dz], rrs.at[e], at(dz, 0, 0))
        rgot.append(copy)
        sends.append(copy)
    my_band = pl.ds(pl.multiple_of((z % NT) * BAND, BAND), BAND)
    rs[0] = part[my_band, :]

    for copy in zgot:
        copy.wait_recv()
    scales = []
    for hh in range(PAIR):
        top = jnp.concatenate([zst[e, hh : hh + 1, :] for e in range(NZ)], axis=0)
        total = jnp.concatenate(
            [zst[e, PAIR + hh : PAIR + hh + 1, :] for e in range(NZ)], axis=0
        )
        highest = jnp.max(top, axis=0, keepdims=True)
        w = jnp.exp(top - highest)
        scales.append(w / jnp.sum(w * total, axis=0, keepdims=True))
    pad = jnp.zeros((ROWS - PAIR * NZ, ROWS), F32)
    scale_t[...] = jnp.transpose(jnp.concatenate(scales + [pad], axis=0))
    mine = scale_t[my_band, :]
    for e in range(NZ):
        for hh in range(PAIR):
            zw[e, :, hh * HD : (hh + 1) * HD] = jnp.broadcast_to(
                mine[:, hh * NZ + e : hh * NZ + e + 1], (BAND, HD)
            )
    for copy in rgot:
        copy.wait_recv()
    acc = jnp.zeros((BAND, PAIR * HD), F32)
    for e in range(NZ):
        acc = acc + rs[e].astype(F32) * zw[e]
    att[my_band, :] = acc.astype(BF16)

    agot = []
    for dz in (4, 3, 13, 2, 14, 1, 15):
        copy = remote(att.at[my_band], att.at[my_band], sag.at[dz], rag.at[dz], at(dz, 0, 0))
        agot.append((dz, copy))
        sends.append(copy)
    c_w.wait()
    for copy in wgot:
        copy.wait_recv()
    for dz, copy in agot:
        band = ((z - dz + NZ) % NZ) % NT
        rows = pl.ds(pl.multiple_of(band * BAND, BAND), BAND)
        pltpu.make_async_copy(att.at[rows], att.at[rows], rag.at[dz]).wait()

    pgot = []
    for dx in (2, 1, 3, 0):
        pl_send[dx] = dot(att[...], wx[dx]).astype(BF16)
        for dt in (4, 5, 3, 2, 6, 1, 7, 0):
            if (dx, dt) == (0, 0):
                continue
            rows = pl.ds(pl.multiple_of(((t + dt) % NT) * BAND, BAND), BAND)
            e = ((NX - dx) % NX) * NT + (NT - dt) % NT
            copy = remote(
                pl_send.at[dx, rows],
                pl_recv.at[e],
                spl.at[dx * NT + dt],
                rpl.at[e],
                at(0, dx, dt),
            )
            pgot.append(copy)
            sends.append(copy)
    rows = pl.ds(pl.multiple_of(t * BAND, BAND), BAND)
    acc = pl_send[0, rows, :].astype(F32)
    for copy in pgot:
        copy.wait_recv()
    for e in range(1, NX * NT):
        acc = acc + pl_recv[e].astype(F32)
    out_ref[...] = acc.astype(BF16)
    for copy in sends:
        copy.wait_send()


def on_device(queries, key_cache, value_cache, out_weight, lengths, block_table):
    q = queries.reshape(2, GROUP, HD).transpose(1, 0, 2).reshape(2 * GROUP, HD)
    hbm = pl.BlockSpec(memory_space=pltpu.HBM)
    dma = pltpu.SemaphoreType.DMA
    vmem = pltpu.VMEM
    return pl.pallas_call(
        kernel,
        out_shape=jax.ShapeDtypeStruct((BAND, HD), BF16),
        in_specs=[hbm] * 6,
        out_specs=pl.BlockSpec(memory_space=pltpu.VMEM),
        scratch_shapes=[
            vmem((MAXB, ROWS), jnp.int32),
            vmem((1, ROWS), jnp.int32),
            vmem((SLOTS, BLK, HD), BF16),
            vmem((SLOTS, BLK, HD), BF16),
            vmem((NX, NZ, 2 * GROUP, HD), BF16),
            vmem((ROWS, ROWS * GROUP), BF16),
            vmem((ROWS, ROWS), F32),
            vmem((NX * SLOTS, ROWS), F32),
            vmem((SLOTS, GROUP, BLK), BF16),
            vmem((ROWS, HD), F32),
            vmem((ROWS, HD), F32),
            vmem((ROWS, HD), BF16),
            vmem((NX, PAIR * SLOTS, HD), F32),
            vmem((NX, PAIR * SLOTS, HD), BF16),
            vmem((8, ROWS), F32),
            vmem((NZ, 8, ROWS), F32),
            vmem((ROWS, ROWS), F32),
            vmem((NZ, BAND, PAIR * HD), F32),
            vmem((ROWS, PAIR * HD), BF16),
            vmem((NZ, BAND, PAIR * HD), BF16),
            vmem((ROWS, PAIR * HD), BF16),
            vmem((NX, PAIR * HD, HD), BF16),
            vmem((NX, ROWS, HD), BF16),
            vmem((NX * NT, BAND, HD), BF16),
            dma((6,)),
            dma((NZ,)),
            dma((NZ,)),
            dma((NX, 2)),
            dma((NX, 2)),
            dma((NX,)),
            dma((NX,)),
            dma((NX,)),
            dma((NX,)),
            dma((NX,)),
            dma((NX,)),
            dma((NZ,)),
            dma((NZ,)),
            dma((NZ,)),
            dma((NZ,)),
            dma((NZ,)),
            dma((NZ,)),
            dma((NX * NT,)),
            dma((NX * NT,)),
        ],
        compiler_params=pltpu.CompilerParams(
            collective_id=0, has_side_effects=True, vmem_limit_bytes=56 * 1024 * 1024
        ),
        cost_estimate=pl.CostEstimate(
            flops=400_000_000, bytes_accessed=5_000_000, transcendentals=70_000
        ),
        name="lent_attention",
    )(q, key_cache, value_cache, out_weight, lengths.reshape(1, ROWS), block_table.T)


def solution(mesh):
    return jax.shard_map(
        on_device,
        mesh=mesh,
        in_specs=(
            P("pool", "tp"),
            P("tp", "pool", None, None),
            P("tp", "pool", None, None),
            P("tp", "pool"),
            P(),
            P(),
        ),
        out_specs=P("tp", "pool"),
        check_vma=False,
    )
```

```python
import functools
import math

import jax
import jax.numpy as jnp
from jax import lax
from jax.experimental import pallas as pl
from jax.experimental.pallas import tpu as pltpu
from jax.sharding import PartitionSpec as P

MESH = pl.DeviceIdType.MESH
FLOOR = -1e30
F32 = jnp.float32
BF16 = jnp.bfloat16

NZ, NX, NT = 16, 4, 8
ROWS, SLOTS, BLK, HD, GROUP, MAXB = 128, 16, 512, 128, 8, 32
PAIR = GROUP // NX
BAND = ROWS // NT
ZORDER = [0, 1, 2, 3, 4, 15, 14, 13, 12, 5, 6, 11, 10, 7, 8, 9]
LEGS = ((0, 9), (9, 13), (13, 16))
FAR_FIRST = (8, 7, 9, 6, 10, 5, 11, 4, 12, 3, 13, 2, 14, 1, 15)
ENDS = sorted(
    [(dz, dx) for dz in range(-3, 5) for dx in range(NX)],
    key=lambda d: -(abs(d[0]) + min(d[1], NX - d[1])),
)


def dot(a, b, dims=((1,), (0,))):
    return lax.dot_general(a, b, (dims, ((), ())), preferred_element_type=F32)


def kernel(
    q_hbm,
    k_hbm,
    v_hbm,
    w_hbm,
    len_hbm,
    tab_hbm,
    out_ref,
    tab,
    lens,
    keys,
    keys_t,
    vals,
    qall,
    sel,
    lims,
    hold,
    score,
    prob,
    o_f,
    stat_f,
    o_send,
    st_x,
    o_x,
    zst_send,
    zst,
    scale_t,
    zw,
    part,
    rs,
    band,
    fin,
    wall,
    loc_sem,
    sq,
    rq,
    sqx,
    rqx,
    sw,
    rw,
    sst,
    rst,
    so,
    ro,
    szs,
    rzs,
    srs,
    rrs,
    sfin,
    rfin,
    seen,
):
    pool = lax.axis_index("pool")
    t = lax.axis_index("tp")
    z = pool // NX
    x = pool % NX
    mine = (z + 3 * t) % NT

    def at(dz, dx):
        return {"pool": ((z + dz) % NZ) * NX + (x + dx) % NX, "tp": t}

    def remote(src, dst, send, recv, to):
        copy = pltpu.make_async_remote_copy(
            src_ref=src,
            dst_ref=dst,
            send_sem=send,
            recv_sem=recv,
            device_id=to,
            device_id_type=MESH,
        )
        copy.start()
        return copy

    def rows_of(index, size):
        return pl.ds(pl.multiple_of(index * size, size), size)

    def arrived(ref, sem):
        pltpu.make_async_copy(ref, ref, sem).wait()

    barrier = pltpu.get_barrier_semaphore()
    for dz in FAR_FIRST:
        pl.semaphore_signal(barrier, inc=1, device_id=at(dz, 0), device_id_type=MESH)
    c_q = pltpu.make_async_copy(q_hbm, qall.at[0, 0], loc_sem.at[2])
    c_q.start()
    for dt in (4, 3, 5, 2, 6, 1, 7):
        pl.semaphore_signal(
            barrier, inc=1, device_id={"pool": pool, "tp": (t + dt) % NT}, device_id_type=MESH
        )
    for dx in (2, 1, 3):
        pl.semaphore_signal(barrier, inc=1, device_id=at(0, dx), device_id_type=MESH)
    c_tab = pltpu.make_async_copy(tab_hbm, tab, loc_sem.at[0])
    c_len = pltpu.make_async_copy(len_hbm, lens, loc_sem.at[1])
    c_k = pltpu.make_async_copy(k_hbm.at[0], keys, loc_sem.at[3])
    c_v = pltpu.make_async_copy(v_hbm.at[0], vals, loc_sem.at[4])
    c_w = pltpu.make_async_copy(w_hbm, wall.at[t], loc_sem.at[5])
    c_tab.start()
    c_len.start()
    c_k.start()
    c_v.start()
    c_w.start()
    c_q.wait()
    pl.semaphore_wait(barrier, NZ - 1 + NX - 1 + NT - 1)

    place = {dz: k for k, dz in enumerate(ZORDER)}
    leg_of = [n for n, (lo, hi) in enumerate(LEGS) for k in range(lo, hi)]
    for dz in FAR_FIRST:
        k = place[NZ - dz]
        remote(qall.at[0, 0], qall.at[0, k], sq, rq.at[leg_of[k]], at(dz, 0))
    sibling = {"pool": pool, "tp": t + 1 - 2 * (t % 2)}
    for dt in (2, 6, 4):
        remote(w_hbm, wall.at[t], sw.at[0], rw.at[0], {"pool": pool, "tp": (t + dt) % NT})
    remote(w_hbm, wall.at[t], sw.at[1], rw.at[1], sibling)

    c_tab.wait()
    c_len.wait()
    tab_t = tab[...].astype(F32)
    len_row = lens[...].astype(F32)
    sub = lax.broadcasted_iota(jnp.int32, (ROWS, ROWS), 0)
    lane = lax.broadcasted_iota(jnp.int32, (ROWS, ROWS), 1)
    sid = (pool * SLOTS + sub // GROUP).astype(F32)
    left = jnp.zeros((ROWS, ROWS), F32)
    sub4 = lax.broadcasted_iota(jnp.int32, (NX * SLOTS, ROWS), 0)
    sid4 = ((z * NX + (x + sub4 // SLOTS) % NX) * SLOTS + sub4 % SLOTS).astype(F32)
    held = jnp.zeros((NX * SLOTS, ROWS), F32)
    for b in range(MAXB):
        entry = tab_t[b : b + 1, :]
        left = jnp.where(entry == sid, len_row - float(BLK * b), left)
        held = jnp.where(entry == sid4, 1.0, held)
    hold[...] = held
    lims[...] = jnp.broadcast_to(jnp.sum(left, axis=1, keepdims=True), (ROWS, ROWS))
    row_of = jnp.sum(
        jnp.where(left > 0.0, (lane + 1).astype(F32), 0.0), axis=1, keepdims=True
    )
    key_col = (row_of - 1.0) * float(GROUP) + (sub[:, 0:1] % GROUP).astype(F32)
    j = lax.broadcasted_iota(jnp.int32, (1, ROWS * GROUP), 1)
    piece = j // (2 * GROUP)
    k_j = piece % NZ
    dz_j = jnp.zeros_like(j)
    for k, dz in enumerate(ZORDER):
        dz_j = jnp.where(k_j == k, dz, dz_j)
    p_j = ((z + dz_j) % NZ) * NX + (x + piece // NZ) % NX
    key_row = ((2 * p_j + j % 2) * GROUP + (j % (2 * GROUP)) // 2).astype(F32)
    for c in range(8):
        cut = slice(c * 128, (c + 1) * 128)
        sel[:, cut] = jnp.where(key_col == key_row[:, cut], 1.0, 0.0).astype(BF16)

    for lo, hi in LEGS:
        new = max(lo, 1)
        arrived(qall.at[0, pl.ds(new, hi - new)], rq.at[LEGS.index((lo, hi))])
        for dx in (2, 1, 3):
            cut = pl.ds(lo, hi - lo)
            remote(qall.at[0, cut], qall.at[(NX - dx) % NX, cut], sqx, rqx, at(0, dx))
    c_k.wait()
    for s in range(SLOTS):
        keys_t[s] = keys[s].T
    arrived(qall.at[pl.ds(1, NX - 1)], rqx)
    teller = 3 * (t - z + NZ) % NT

    @pl.when(teller != t)
    def _():
        pl.semaphore_signal(
            seen, inc=1, device_id={"pool": pool, "tp": teller}, device_id_type=MESH
        )

    picked = dot(sel[...], qall[...].reshape(ROWS * GROUP, HD))
    scaling = 1.0 / math.sqrt(HD)
    for s in range(SLOTS):
        cut = slice(GROUP * s, GROUP * (s + 1))
        score[cut] = dot(picked[cut].astype(BF16), keys_t[s])
    each = 4
    place_in = lax.broadcasted_iota(jnp.int32, (each * GROUP, BLK), 1).astype(F32)
    first = lax.broadcasted_iota(jnp.int32, (GROUP, HD), 1) == 0
    for c in range(SLOTS // each):
        cut = slice(each * GROUP * c, each * GROUP * (c + 1))
        usable = place_in < lims[cut, 0:1]
        scores = jnp.where(usable, score[cut] * scaling, FLOOR)
        peak = jnp.max(scores, axis=1, keepdims=True)
        weights = jnp.where(usable, jnp.exp(scores - peak), 0.0)
        total = jnp.sum(weights, axis=1, keepdims=True)
        for i in range(each):
            s = each * c + i
            sl = slice(GROUP * i, GROUP * (i + 1))
            prob[s] = weights[sl].astype(BF16)
            stat_f[pl.ds(s, GROUP, stride=SLOTS), :] = jnp.where(first, peak[sl], total[sl])
    mine_x = rows_of(x, PAIR * SLOTS)
    for dx in (2, 1, 3):
        rows = rows_of((x + dx) % NX, PAIR * SLOTS)
        remote(stat_f.at[rows], st_x.at[(NX - dx) % NX], sst, rst, at(0, dx))
    st_x[0] = stat_f[mine_x, :]
    c_v.wait()
    for s in range(SLOTS):
        o_f[pl.ds(s, GROUP, stride=SLOTS), :] = dot(prob[s], vals[s])
    o_send[...] = o_f[...].astype(BF16)
    for dx in (2, 1, 3):
        rows = rows_of((x + dx) % NX, PAIR * SLOTS)
        remote(o_send.at[rows], o_x.at[(NX - dx) % NX], so, ro, at(0, dx))
    o_x[0] = o_send[mine_x, :]

    arrived(st_x.at[pl.ds(1, NX - 1)], rst)
    ws = []
    is_held = hold[...] > 0.0
    for hh in range(PAIR):
        cut = slice(hh * SLOTS, (hh + 1) * SLOTS)
        peak = jnp.concatenate([st_x[e, cut, 0:1] for e in range(NX)], axis=0)
        total = jnp.concatenate([st_x[e, cut, 1:2] for e in range(NX)], axis=0)
        top = jnp.max(jnp.where(is_held, peak, FLOOR), axis=0, keepdims=True)
        w = jnp.where(is_held, jnp.exp(peak - top), 0.0)
        coarse = w.astype(BF16)
        ws.append((coarse, (w - coarse.astype(F32)).astype(BF16)))
        zst_send[hh : hh + 1, :] = top
        zst_send[PAIR + hh : PAIR + hh + 1, :] = jnp.sum(w * total, axis=0, keepdims=True)
    for dz in FAR_FIRST:
        remote(zst_send, zst.at[NZ - dz], szs, rzs, at(dz, 0))
    zst[0] = zst_send[...]

    arrived(o_x.at[pl.ds(1, NX - 1)], ro)
    for hh in range(PAIR):
        data = jnp.concatenate(
            [o_x[e, hh * SLOTS : (hh + 1) * SLOTS, :] for e in range(NX)], axis=0
        )
        both = dot(ws[hh][0], data, ((0,), (0,))) + dot(ws[hh][1], data, ((0,), (0,)))
        part[:, hh * HD : (hh + 1) * HD] = both.astype(BF16)
    for dz in FAR_FIRST:
        remote(part.at[rows_of((mine + dz) % NT, BAND)], rs.at[NZ - dz], srs, rrs, at(dz, 0))
    my_band = rows_of(mine, BAND)
    rs[0] = part[my_band, :]

    arrived(wall.at[pl.ds(0, 3)], rw.at[0])
    for dt in (2, 6, 4):
        origin = (t + dt) % NT
        remote(wall.at[origin], wall.at[origin], sw.at[1], rw.at[1], sibling)

    arrived(qall.at[0, pl.ds(0, NZ - 1)], sq)
    arrived(qall.at[pl.ds(0, NX - 1)], sqx)
    arrived(wall.at[pl.ds(0, 3)], sw.at[0])
    arrived(st_x.at[pl.ds(0, NX - 1)], sst)
    arrived(o_x.at[pl.ds(0, NX - 1)], so)
    arrived(zst.at[pl.ds(0, NZ - 1)], szs)

    arrived(zst.at[pl.ds(1, NZ - 1)], rzs)
    scales = []
    for hh in range(PAIR):
        top = jnp.concatenate([zst[e, hh : hh + 1, :] for e in range(NZ)], axis=0)
        total = jnp.concatenate(
            [zst[e, PAIR + hh : PAIR + hh + 1, :] for e in range(NZ)], axis=0
        )
        highest = jnp.max(top, axis=0, keepdims=True)
        w = jnp.exp(top - highest)
        scales.append(w / jnp.sum(w * total, axis=0, keepdims=True))
    pad = jnp.zeros((ROWS - PAIR * NZ, ROWS), F32)
    scale_t[...] = jnp.transpose(jnp.concatenate(scales + [pad], axis=0))
    cols = scale_t[my_band, :]
    for e in range(NZ):
        for hh in range(PAIR):
            zw[e, :, hh * HD : (hh + 1) * HD] = jnp.broadcast_to(
                cols[:, hh * NZ + e : hh * NZ + e + 1], (BAND, HD)
            )
    arrived(rs.at[pl.ds(1, NZ - 1)], rrs)
    acc = jnp.zeros((BAND, PAIR * HD), F32)
    for e in range(NZ):
        acc = acc + rs[e].astype(F32) * zw[e]
    band[...] = acc.astype(BF16)

    @pl.when(mine != t)
    def _():
        pl.semaphore_wait(seen, 1)

    origin = t * NX + x
    along = 1 - 2 * (t % 2)

    def end(dz, dx):
        to = at(along * dz + NZ, dx)
        to["tp"] = mine
        return pltpu.make_async_remote_copy(
            src_ref=band,
            dst_ref=fin.at[origin],
            send_sem=sfin,
            recv_sem=rfin,
            device_id=to,
            device_id_type=MESH,
        )

    for dz, dx in ENDS:
        if (dz, dx) == (0, 0):

            @pl.when(mine != t)
            def _():
                end(0, 0).start()

            @pl.when(mine == t)
            def _():
                pltpu.make_async_copy(band, fin.at[origin], rfin).start()
        else:
            end(dz, dx).start()
    arrived(rs.at[pl.ds(0, NZ - 1)], srs)

    c_w.wait()
    arrived(wall.at[pl.ds(0, NX)], rw.at[1])
    arrived(wall.at[pl.ds(0, NX)], sw.at[1])
    arrived(fin, rfin)
    acc = jnp.zeros((BAND, HD), F32)
    for n in range(NT * NX):
        cut = slice((n % NX) * PAIR * HD, (n % NX + 1) * PAIR * HD)
        acc = acc + dot(fin[n], wall[n // NX, cut, :])
    out_ref[...] = acc.astype(BF16)
    arrived(fin.at[pl.ds(0, len(ENDS) - 1)], sfin)

    @pl.when(mine != t)
    def _():
        end(0, 0).wait_send()


def on_device(queries, key_cache, value_cache, out_weight, lengths, block_table):
    q = queries.reshape(2, GROUP, HD).transpose(1, 0, 2).reshape(2 * GROUP, HD)
    hbm = pl.BlockSpec(memory_space=pltpu.HBM)
    dma = pltpu.SemaphoreType.DMA
    vmem = pltpu.VMEM
    return pl.pallas_call(
        kernel,
        out_shape=jax.ShapeDtypeStruct((BAND, HD), BF16),
        in_specs=[hbm] * 6,
        out_specs=pl.BlockSpec(memory_space=pltpu.VMEM),
        scratch_shapes=[
            vmem((MAXB, ROWS), jnp.int32),
            vmem((1, ROWS), jnp.int32),
            vmem((SLOTS, BLK, HD), BF16),
            vmem((SLOTS, HD, BLK), BF16),
            vmem((SLOTS, BLK, HD), BF16),
            vmem((NX, NZ, 2 * GROUP, HD), BF16),
            vmem((ROWS, ROWS * GROUP), BF16),
            vmem((ROWS, ROWS), F32),
            vmem((NX * SLOTS, ROWS), F32),
            vmem((ROWS, BLK), F32),
            vmem((SLOTS, GROUP, BLK), BF16),
            vmem((ROWS, HD), F32),
            vmem((ROWS, HD), F32),
            vmem((ROWS, HD), BF16),
            vmem((NX, PAIR * SLOTS, HD), F32),
            vmem((NX, PAIR * SLOTS, HD), BF16),
            vmem((8, ROWS), F32),
            vmem((NZ, 8, ROWS), F32),
            vmem((ROWS, ROWS), F32),
            vmem((NZ, BAND, PAIR * HD), F32),
            vmem((ROWS, PAIR * HD), BF16),
            vmem((NZ, BAND, PAIR * HD), BF16),
            vmem((BAND, PAIR * HD), BF16),
            vmem((NT * NX, BAND, PAIR * HD), BF16),
            vmem((NT, GROUP * HD, HD), BF16),
            dma((6,)),
            dma,
            dma((len(LEGS),)),
            dma,
            dma,
            dma((2,)),
            dma((2,)),
            dma,
            dma,
            dma,
            dma,
            dma,
            dma,
            dma,
            dma,
            dma,
            dma,
            pltpu.SemaphoreType.REGULAR,
        ],
        compiler_params=pltpu.CompilerParams(
            collective_id=0, has_side_effects=True, vmem_limit_bytes=56 * 1024 * 1024
        ),
        cost_estimate=pl.CostEstimate(
            flops=400_000_000, bytes_accessed=5_000_000, transcendentals=70_000
        ),
        name="lent_attention",
    )(q, key_cache, value_cache, out_weight, lengths.reshape(1, ROWS), block_table.T)


def solution(mesh):
    return jax.shard_map(
        on_device,
        mesh=mesh,
        in_specs=(
            P("pool", "tp"),
            P("tp", "pool", None, None),
            P("tp", "pool", None, None),
            P("tp", "pool"),
            P(),
            P(),
        ),
        out_specs=P("tp", "pool"),
        check_vma=False,
    )
```

```python
import functools
import math

import jax
import jax.numpy as jnp
from jax import lax
from jax.experimental import pallas as pl
from jax.experimental.pallas import tpu as pltpu
from jax.sharding import PartitionSpec as P

MESH = pl.DeviceIdType.MESH
FLOOR = -1e30
F32 = jnp.float32
BF16 = jnp.bfloat16

NZ, NX, NT = 16, 4, 8
ROWS, SLOTS, BLK, HD, GROUP, MAXB = 128, 16, 512, 128, 8, 32
PAIR = GROUP // NX
BAND = ROWS // NT
ZORDER = [0, 1, 2, 3, 4, 15, 14, 13, 12, 5, 6, 11, 10, 7, 8, 9]
LEGS = ((0, 9), (9, 13), (13, 16))
FAR_FIRST = (8, 7, 9, 6, 10, 5, 11, 4, 12, 3, 13, 2, 14, 1, 15)
ENDS = sorted(
    [(dz, dx) for dz in range(-3, 5) for dx in range(NX)],
    key=lambda d: -(abs(d[0]) + min(d[1], NX - d[1])),
)


def dot(a, b, dims=((1,), (0,))):
    return lax.dot_general(a, b, (dims, ((), ())), preferred_element_type=F32)


def kernel(
    q_hbm,
    k_hbm,
    v_hbm,
    w_hbm,
    len_hbm,
    tab_hbm,
    out_ref,
    tab,
    lens,
    keys,
    keys_t,
    vals,
    qall,
    sel,
    lims,
    hold,
    score,
    prob,
    o_f,
    stat_f,
    o_send,
    st_send,
    st_x,
    o_x,
    zst_send,
    zst,
    scale_t,
    zw,
    part,
    rs,
    band,
    fin,
    wall,
    loc_sem,
    sq,
    rq,
    sqx,
    rqx,
    sw,
    rw,
    sst,
    rst,
    so,
    ro,
    szs,
    rzs,
    srs,
    rrs,
    sfin,
    rfin,
    seen,
):
    pool = lax.axis_index("pool")
    t = lax.axis_index("tp")
    z = pool // NX
    x = pool % NX
    mine = (z + 3 * t) % NT

    def at(dz, dx):
        return {"pool": ((z + dz) % NZ) * NX + (x + dx) % NX, "tp": t}

    def remote(src, dst, send, recv, to):
        copy = pltpu.make_async_remote_copy(
            src_ref=src,
            dst_ref=dst,
            send_sem=send,
            recv_sem=recv,
            device_id=to,
            device_id_type=MESH,
        )
        copy.start()
        return copy

    def rows_of(index, size):
        return pl.ds(pl.multiple_of(index * size, size), size)

    def arrived(ref, sem):
        pltpu.make_async_copy(ref, ref, sem).wait()

    barrier = pltpu.get_barrier_semaphore()
    for dz in FAR_FIRST:
        pl.semaphore_signal(barrier, inc=1, device_id=at(dz, 0), device_id_type=MESH)
    c_q = pltpu.make_async_copy(q_hbm, qall.at[0, 0], loc_sem.at[2])
    c_q.start()
    for dt in (4, 3, 5, 2, 6, 1, 7):
        pl.semaphore_signal(
            barrier, inc=1, device_id={"pool": pool, "tp": (t + dt) % NT}, device_id_type=MESH
        )
    for dx in (2, 1, 3):
        pl.semaphore_signal(barrier, inc=1, device_id=at(0, dx), device_id_type=MESH)
    c_tab = pltpu.make_async_copy(tab_hbm, tab, loc_sem.at[0])
    c_len = pltpu.make_async_copy(len_hbm, lens, loc_sem.at[1])
    c_k = pltpu.make_async_copy(k_hbm.at[0], keys, loc_sem.at[3])
    c_v = pltpu.make_async_copy(v_hbm.at[0], vals, loc_sem.at[4])
    c_w = pltpu.make_async_copy(w_hbm, wall.at[t], loc_sem.at[5])
    c_tab.start()
    c_len.start()
    c_k.start()
    c_v.start()
    c_w.start()
    c_q.wait()
    pl.semaphore_wait(barrier, NZ - 1 + NX - 1 + NT - 1)

    place = {dz: k for k, dz in enumerate(ZORDER)}
    leg_of = [n for n, (lo, hi) in enumerate(LEGS) for k in range(lo, hi)]
    for dz in FAR_FIRST:
        k = place[NZ - dz]
        remote(qall.at[0, 0], qall.at[0, k], sq, rq.at[leg_of[k]], at(dz, 0))
    sibling = {"pool": pool, "tp": t + 1 - 2 * (t % 2)}
    for dt in (2, 6, 4):
        remote(w_hbm, wall.at[t], sw.at[0], rw.at[0], {"pool": pool, "tp": (t + dt) % NT})
    remote(w_hbm, wall.at[t], sw.at[1], rw.at[1], sibling)

    c_tab.wait()
    c_len.wait()
    tab_t = tab[...].astype(F32)
    len_row = lens[...].astype(F32)
    sub = lax.broadcasted_iota(jnp.int32, (ROWS, ROWS), 0)
    lane = lax.broadcasted_iota(jnp.int32, (ROWS, ROWS), 1)
    sid = (pool * SLOTS + sub // GROUP).astype(F32)
    left = jnp.zeros((ROWS, ROWS), F32)
    sub4 = lax.broadcasted_iota(jnp.int32, (NX * SLOTS, ROWS), 0)
    sid4 = ((z * NX + (x + sub4 // SLOTS) % NX) * SLOTS + sub4 % SLOTS).astype(F32)
    held = jnp.zeros((NX * SLOTS, ROWS), F32)
    for b in range(MAXB):
        entry = tab_t[b : b + 1, :]
        left = jnp.where(entry == sid, len_row - float(BLK * b), left)
        held = jnp.where(entry == sid4, 1.0, held)
    hold[...] = held
    lims[...] = jnp.broadcast_to(jnp.sum(left, axis=1, keepdims=True), (ROWS, ROWS))
    row_of = jnp.sum(
        jnp.where(left > 0.0, (lane + 1).astype(F32), 0.0), axis=1, keepdims=True
    )
    key_col = (row_of - 1.0) * float(GROUP) + (sub[:, 0:1] % GROUP).astype(F32)
    j = lax.broadcasted_iota(jnp.int32, (1, ROWS * GROUP), 1)
    piece = j // (2 * GROUP)
    k_j = piece % NZ
    dz_j = jnp.zeros_like(j)
    for k, dz in enumerate(ZORDER):
        dz_j = jnp.where(k_j == k, dz, dz_j)
    p_j = ((z + dz_j) % NZ) * NX + (x + piece // NZ) % NX
    key_row = ((2 * p_j + j % 2) * GROUP + (j % (2 * GROUP)) // 2).astype(F32)
    for c in range(8):
        cut = slice(c * 128, (c + 1) * 128)
        sel[:, cut] = jnp.where(key_col == key_row[:, cut], 1.0, 0.0).astype(BF16)

    for lo, hi in LEGS:
        new = max(lo, 1)
        arrived(qall.at[0, pl.ds(new, hi - new)], rq.at[LEGS.index((lo, hi))])
        for dx in (2, 1, 3):
            cut = pl.ds(lo, hi - lo)
            remote(qall.at[0, cut], qall.at[(NX - dx) % NX, cut], sqx, rqx, at(0, dx))
    c_k.wait()
    for s in range(SLOTS):
        keys_t[s] = keys[s].T
    arrived(qall.at[pl.ds(1, NX - 1)], rqx)
    teller = 3 * (t - z + NZ) % NT

    @pl.when(teller != t)
    def _():
        pl.semaphore_signal(
            seen, inc=1, device_id={"pool": pool, "tp": teller}, device_id_type=MESH
        )

    picked = dot(sel[...], qall[...].reshape(ROWS * GROUP, HD))
    scaling = 1.0 / math.sqrt(HD)
    for s in range(SLOTS):
        cut = slice(GROUP * s, GROUP * (s + 1))
        score[cut] = dot(picked[cut].astype(BF16), keys_t[s])
    each = 4
    place_in = lax.broadcasted_iota(jnp.int32, (each * GROUP, BLK), 1).astype(F32)
    inverse = []
    for c in range(SLOTS // each):
        cut = slice(each * GROUP * c, each * GROUP * (c + 1))
        usable = place_in < lims[cut, 0:1]
        scores = jnp.where(usable, score[cut] * scaling, FLOOR)
        peak = jnp.max(scores, axis=1, keepdims=True)
        weights = jnp.where(usable, jnp.exp(scores - peak), 0.0)
        total = jnp.sum(weights, axis=1, keepdims=True)
        used = total > 0.0
        inverse.append(jnp.where(used, 1.0 / jnp.where(used, total, 1.0), 0.0))
        level = jnp.where(used, peak + jnp.log(jnp.where(used, total, 1.0)), FLOOR)
        for i in range(each):
            s = each * c + i
            sl = slice(GROUP * i, GROUP * (i + 1))
            prob[s] = weights[sl].astype(BF16)
            stat_f[pl.ds(s, GROUP, stride=SLOTS), :] = jnp.broadcast_to(level[sl], (GROUP, HD))
    mine_x = rows_of(x, PAIR * SLOTS)
    st_send[...] = jnp.transpose(stat_f[...])[0:1, :]
    for dx in (2, 1, 3):
        remote(st_send, st_x.at[(NX - dx) % NX], sst, rst, at(0, dx))
    st_x[0] = st_send[...]
    c_v.wait()
    for s in range(SLOTS):
        sl = slice(GROUP * (s % each), GROUP * (s % each + 1))
        o_f[pl.ds(s, GROUP, stride=SLOTS), :] = dot(prob[s], vals[s]) * inverse[s // each][sl]
    o_send[...] = o_f[...].astype(BF16)
    for dx in (2, 1, 3):
        rows = rows_of((x + dx) % NX, PAIR * SLOTS)
        remote(o_send.at[rows], o_x.at[(NX - dx) % NX], so, ro, at(0, dx))
    o_x[0] = o_send[mine_x, :]

    arrived(st_x.at[pl.ds(1, NX - 1)], rst)
    pad = jnp.zeros((ROWS - NX, ROWS), F32)
    stat_f[...] = jnp.transpose(jnp.concatenate([st_x[e] for e in range(NX)] + [pad], axis=0))
    own = stat_f[mine_x, :]
    ws = []
    is_held = hold[...] > 0.0
    for hh in range(PAIR):
        cut = slice(hh * SLOTS, (hh + 1) * SLOTS)
        level = jnp.concatenate([own[cut, e : e + 1] for e in range(NX)], axis=0)
        top = jnp.max(jnp.where(is_held, level, FLOOR), axis=0, keepdims=True)
        w = jnp.where(is_held, jnp.exp(level - top), 0.0)
        total = jnp.sum(w, axis=0, keepdims=True)
        used = total > 0.0
        total = jnp.where(used, total, 1.0)
        w = w / total
        coarse = w.astype(BF16)
        ws.append((coarse, (w - coarse.astype(F32)).astype(BF16)))
        zst_send[hh : hh + 1, :] = jnp.where(used, top + jnp.log(total), FLOOR)
    for dz in FAR_FIRST:
        remote(zst_send, zst.at[NZ - dz], szs, rzs, at(dz, 0))
    zst[0] = zst_send[...]

    arrived(o_x.at[pl.ds(1, NX - 1)], ro)
    for hh in range(PAIR):
        data = jnp.concatenate(
            [o_x[e, hh * SLOTS : (hh + 1) * SLOTS, :] for e in range(NX)], axis=0
        )
        both = dot(ws[hh][0], data, ((0,), (0,))) + dot(ws[hh][1], data, ((0,), (0,)))
        part[:, hh * HD : (hh + 1) * HD] = both.astype(BF16)
    for dz in FAR_FIRST:
        remote(part.at[rows_of((mine + dz) % NT, BAND)], rs.at[NZ - dz], srs, rrs, at(dz, 0))
    my_band = rows_of(mine, BAND)
    rs[0] = part[my_band, :]

    arrived(wall.at[pl.ds(0, 3)], rw.at[0])
    for dt in (2, 6, 4):
        origin = (t + dt) % NT
        remote(wall.at[origin], wall.at[origin], sw.at[1], rw.at[1], sibling)

    arrived(qall.at[0, pl.ds(0, NZ - 1)], sq)
    arrived(qall.at[pl.ds(0, NX - 1)], sqx)
    arrived(wall.at[pl.ds(0, 3)], sw.at[0])
    arrived(st_x.at[pl.ds(0, NX - 1)], sst)
    arrived(o_x.at[pl.ds(0, NX - 1)], so)
    arrived(zst.at[pl.ds(0, NZ - 1)], szs)

    arrived(zst.at[pl.ds(1, NZ - 1)], rzs)
    scales = []
    for hh in range(PAIR):
        level = jnp.concatenate([zst[e, hh : hh + 1, :] for e in range(NZ)], axis=0)
        w = jnp.exp(level - jnp.max(level, axis=0, keepdims=True))
        scales.append(w / jnp.sum(w, axis=0, keepdims=True))
    pad = jnp.zeros((ROWS - PAIR * NZ, ROWS), F32)
    scale_t[...] = jnp.transpose(jnp.concatenate(scales + [pad], axis=0))
    cols = scale_t[my_band, :]
    for e in range(NZ):
        for hh in range(PAIR):
            zw[e, :, hh * HD : (hh + 1) * HD] = jnp.broadcast_to(
                cols[:, hh * NZ + e : hh * NZ + e + 1], (BAND, HD)
            )
    arrived(rs.at[pl.ds(1, NZ - 1)], rrs)
    acc = jnp.zeros((BAND, PAIR * HD), F32)
    for e in range(NZ):
        acc = acc + rs[e].astype(F32) * zw[e]
    band[...] = acc.astype(BF16)

    @pl.when(mine != t)
    def _():
        pl.semaphore_wait(seen, 1)

    along = 1 - 2 * (t % 2)

    def end(dz, dx):
        to = at(along * dz + NZ, dx)
        to["tp"] = mine
        return pltpu.make_async_remote_copy(
            src_ref=band,
            dst_ref=fin.at[(NX - dx) % NX, t],
            send_sem=sfin,
            recv_sem=rfin.at[(NX - dx) % NX],
            device_id=to,
            device_id_type=MESH,
        )

    for dz, dx in ENDS:
        if (dz, dx) == (0, 0):

            @pl.when(mine != t)
            def _():
                end(0, 0).start()

            @pl.when(mine == t)
            def _():
                pltpu.make_async_copy(band, fin.at[0, t], rfin.at[0]).start()
        else:
            end(dz, dx).start()
    arrived(rs.at[pl.ds(0, NZ - 1)], srs)

    c_w.wait()
    arrived(wall.at[pl.ds(0, NX)], rw.at[1])
    arrived(wall.at[pl.ds(0, NX)], sw.at[1])
    acc = jnp.zeros((BAND, HD), F32)
    for e in (0, 1, 3, 2):
        arrived(fin.at[e], rfin.at[e])
        rows = rows_of((x + e) % NX, PAIR * HD)
        for n in range(NT):
            acc = acc + dot(fin[e, n], wall[n, rows, :])
    out_ref[...] = acc.astype(BF16)
    arrived(fin.at[pl.ds(0, NX - 1)], sfin)
    arrived(fin.at[0, pl.ds(0, NT - 1)], sfin)

    @pl.when(mine != t)
    def _():
        end(0, 0).wait_send()


def on_device(queries, key_cache, value_cache, out_weight, lengths, block_table):
    q = queries.reshape(2, GROUP, HD).transpose(1, 0, 2).reshape(2 * GROUP, HD)
    hbm = pl.BlockSpec(memory_space=pltpu.HBM)
    dma = pltpu.SemaphoreType.DMA
    vmem = pltpu.VMEM
    return pl.pallas_call(
        kernel,
        out_shape=pltpu.VMEM((BAND, HD), BF16),
        in_specs=[hbm] * 6,
        out_specs=pl.BlockSpec(memory_space=pltpu.VMEM),
        scratch_shapes=[
            vmem((MAXB, ROWS), jnp.int32),
            vmem((1, ROWS), jnp.int32),
            vmem((SLOTS, BLK, HD), BF16),
            vmem((SLOTS, HD, BLK), BF16),
            vmem((SLOTS, BLK, HD), BF16),
            vmem((NX, NZ, 2 * GROUP, HD), BF16),
            vmem((ROWS, ROWS * GROUP), BF16),
            vmem((ROWS, ROWS), F32),
            vmem((NX * SLOTS, ROWS), F32),
            vmem((ROWS, BLK), F32),
            vmem((SLOTS, GROUP, BLK), BF16),
            vmem((ROWS, HD), F32),
            vmem((ROWS, HD), F32),
            vmem((ROWS, HD), BF16),
            vmem((1, ROWS), F32),
            vmem((NX, 1, ROWS), F32),
            vmem((NX, PAIR * SLOTS, HD), BF16),
            vmem((PAIR, ROWS), F32),
            vmem((NZ, PAIR, ROWS), F32),
            vmem((ROWS, ROWS), F32),
            vmem((NZ, BAND, PAIR * HD), F32),
            vmem((ROWS, PAIR * HD), BF16),
            vmem((NZ, BAND, PAIR * HD), BF16),
            vmem((BAND, PAIR * HD), BF16),
            vmem((NX, NT, BAND, PAIR * HD), BF16),
            vmem((NT, GROUP * HD, HD), BF16),
            dma((6,)),
            dma,
            dma((len(LEGS),)),
            dma,
            dma,
            dma((2,)),
            dma((2,)),
            dma,
            dma,
            dma,
            dma,
            dma,
            dma,
            dma,
            dma,
            dma,
            dma((NX,)),
            pltpu.SemaphoreType.REGULAR,
        ],
        compiler_params=pltpu.CompilerParams(
            collective_id=0, has_side_effects=True, vmem_limit_bytes=56 * 1024 * 1024
        ),
        cost_estimate=pl.CostEstimate(
            flops=400_000_000, bytes_accessed=5_000_000, transcendentals=70_000
        ),
        name="lent_attention",
    )(q, key_cache, value_cache, out_weight, lengths.reshape(1, ROWS), block_table.T)


def solution(mesh):
    return jax.shard_map(
        on_device,
        mesh=mesh,
        in_specs=(
            P("pool", "tp"),
            P("tp", "pool", None, None),
            P("tp", "pool", None, None),
            P("tp", "pool"),
            P(),
            P(),
        ),
        out_specs=P("tp", "pool"),
        check_vma=False,
    )
```

```python
import functools
import math

import jax
import jax.numpy as jnp
from jax import lax
from jax.experimental import pallas as pl
from jax.experimental.pallas import tpu as pltpu
from jax.sharding import PartitionSpec as P

MESH = pl.DeviceIdType.MESH
FLOOR = -1e30
F32 = jnp.float32
BF16 = jnp.bfloat16

NZ, NX, NT = 16, 4, 8
ROWS, SLOTS, BLK, HD, GROUP, MAXB = 128, 16, 512, 128, 8, 32
PAIR = GROUP // NX
BAND = ROWS // NT
ZORDER = [0, 1, 2, 15, 14, 3, 4, 13, 12, 5, 6, 11, 10, 7, 8, 9]
LEGS = ((0, 5), (5, 9), (9, 13), (13, 16))
FAR_FIRST = (8, 7, 9, 6, 10, 5, 11, 4, 12, 3, 13, 2, 14, 1, 15)

def dot(a, b, dims=((1,), (0,))):
    return lax.dot_general(a, b, (dims, ((), ())), preferred_element_type=F32)


def kernel(
    q_hbm,
    k_hbm,
    v_hbm,
    w_hbm,
    len_hbm,
    tab_hbm,
    out_ref,
    tab,
    lens,
    keys,
    keys_t,
    vals,
    qall,
    sel,
    lims,
    hold,
    score,
    prob,
    o_f,
    stat_f,
    o_send,
    st_send,
    st_x,
    o_x,
    zst_send,
    zst,
    scale_t,
    zw,
    part,
    rs,
    band,
    fin,
    wall,
    loc_sem,
    sq,
    rq,
    sqx,
    rqx,
    sw,
    rw,
    sst,
    rst,
    so,
    ro,
    szs,
    rzs,
    srs,
    rrs,
    sfin,
    rfin,
    seen,
):
    pool = lax.axis_index("pool")
    t = lax.axis_index("tp")
    z = pool // NX
    x = pool % NX
    mine = (z + 3 * t) % NT

    def at(dz, dx):
        return {"pool": ((z + dz) % NZ) * NX + (x + dx) % NX, "tp": t}

    def remote(src, dst, send, recv, to):
        copy = pltpu.make_async_remote_copy(
            src_ref=src,
            dst_ref=dst,
            send_sem=send,
            recv_sem=recv,
            device_id=to,
            device_id_type=MESH,
        )
        copy.start()
        return copy

    def rows_of(index, size):
        return pl.ds(pl.multiple_of(index * size, size), size)

    def arrived(ref, sem):
        pltpu.make_async_copy(ref, ref, sem).wait()

    barrier = pltpu.get_barrier_semaphore()
    for dz in FAR_FIRST:
        pl.semaphore_signal(barrier, inc=1, device_id=at(dz, 0), device_id_type=MESH)
    c_q = pltpu.make_async_copy(q_hbm, qall.at[0, 0], loc_sem.at[2])
    c_q.start()
    for dt in (4, 3, 5, 2, 6, 1, 7):
        pl.semaphore_signal(
            barrier, inc=1, device_id={"pool": pool, "tp": (t + dt) % NT}, device_id_type=MESH
        )
    for dx in (2, 1, 3):
        pl.semaphore_signal(barrier, inc=1, device_id=at(0, dx), device_id_type=MESH)
    c_tab = pltpu.make_async_copy(tab_hbm, tab, loc_sem.at[0])
    c_len = pltpu.make_async_copy(len_hbm, lens, loc_sem.at[1])
    c_k = pltpu.make_async_copy(k_hbm.at[0], keys, loc_sem.at[3])
    c_v = pltpu.make_async_copy(v_hbm.at[0], vals, loc_sem.at[4])
    c_w = pltpu.make_async_copy(w_hbm, wall.at[t], loc_sem.at[5])
    c_tab.start()
    c_len.start()
    c_k.start()
    c_v.start()
    c_w.start()
    c_q.wait()
    pl.semaphore_wait(barrier, NZ - 1 + NX - 1 + NT - 1)

    place = {dz: k for k, dz in enumerate(ZORDER)}
    leg_of = [n for n, (lo, hi) in enumerate(LEGS) for k in range(lo, hi)]
    for dz in FAR_FIRST:
        k = place[NZ - dz]
        remote(qall.at[0, 0], qall.at[0, k], sq, rq.at[leg_of[k]], at(dz, 0))
    c_tab.wait()
    c_len.wait()
    tab_t = tab[...].astype(F32)
    len_row = lens[...].astype(F32)
    sub = lax.broadcasted_iota(jnp.int32, (ROWS, ROWS), 0)
    lane = lax.broadcasted_iota(jnp.int32, (ROWS, ROWS), 1)
    sid = (pool * SLOTS + sub // GROUP).astype(F32)
    left = jnp.zeros((ROWS, ROWS), F32)
    sub4 = lax.broadcasted_iota(jnp.int32, (NX * SLOTS, ROWS), 0)
    sid4 = ((z * NX + (x + sub4 // SLOTS) % NX) * SLOTS + sub4 % SLOTS).astype(F32)
    held = jnp.zeros((NX * SLOTS, ROWS), F32)
    for b in range(MAXB):
        entry = tab_t[b : b + 1, :]
        left = jnp.where(entry == sid, len_row - float(BLK * b), left)
        held = jnp.where(entry == sid4, 1.0, held)
    hold[...] = held
    lims[...] = jnp.broadcast_to(jnp.sum(left, axis=1, keepdims=True), (ROWS, ROWS))
    row_of = jnp.sum(
        jnp.where(left > 0.0, (lane + 1).astype(F32), 0.0), axis=1, keepdims=True
    )
    key_col = (row_of - 1.0) * float(GROUP) + (sub[:, 0:1] % GROUP).astype(F32)
    j = lax.broadcasted_iota(jnp.int32, (1, ROWS * GROUP), 1)
    piece = j // (2 * GROUP)
    k_j = piece % NZ
    dz_j = jnp.zeros_like(j)
    for k, dz in enumerate(ZORDER):
        dz_j = jnp.where(k_j == k, dz, dz_j)
    p_j = ((z + dz_j) % NZ) * NX + (x + piece // NZ) % NX
    key_row = ((2 * p_j + j % 2) * GROUP + (j % (2 * GROUP)) // 2).astype(F32)
    for c in range(8):
        cut = slice(c * 128, (c + 1) * 128)
        sel[:, cut] = jnp.where(key_col == key_row[:, cut], 1.0, 0.0).astype(BF16)

    for lo, hi in LEGS:
        new = max(lo, 1)
        arrived(qall.at[0, pl.ds(new, hi - new)], rq.at[LEGS.index((lo, hi))])
        for dx in (2, 1, 3):
            cut = pl.ds(lo, hi - lo)
            remote(qall.at[0, cut], qall.at[(NX - dx) % NX, cut], sqx, rqx, at(0, dx))
    sibling = {"pool": pool, "tp": t + 1 - 2 * (t % 2)}
    for dt in (2, 6, 4):
        remote(w_hbm, wall.at[t], sw.at[0], rw.at[0], {"pool": pool, "tp": (t + dt) % NT})
    remote(w_hbm, wall.at[t], sw.at[1], rw.at[1], sibling)

    c_k.wait()
    for s in range(SLOTS):
        keys_t[s] = keys[s].T
    arrived(qall.at[pl.ds(1, NX - 1)], rqx)
    teller = 3 * (t - z + NZ) % NT

    @pl.when(teller != t)
    def _():
        pl.semaphore_signal(
            seen, inc=1, device_id={"pool": pool, "tp": teller}, device_id_type=MESH
        )

    picked = dot(sel[...], qall[...].reshape(ROWS * GROUP, HD))
    scaling = 1.0 / math.sqrt(HD)
    for s in range(SLOTS):
        cut = slice(GROUP * s, GROUP * (s + 1))
        score[cut] = dot(picked[cut].astype(BF16), keys_t[s])
    each = 4
    place_in = lax.broadcasted_iota(jnp.int32, (each * GROUP, BLK), 1).astype(F32)
    inverse = []
    for c in range(SLOTS // each):
        cut = slice(each * GROUP * c, each * GROUP * (c + 1))
        usable = place_in < lims[cut, 0:1]
        scores = jnp.where(usable, score[cut] * scaling, FLOOR)
        peak = jnp.max(scores, axis=1, keepdims=True)
        weights = jnp.where(usable, jnp.exp(scores - peak), 0.0)
        total = jnp.sum(weights, axis=1, keepdims=True)
        used = total > 0.0
        inverse.append(jnp.where(used, 1.0 / jnp.where(used, total, 1.0), 0.0))
        level = jnp.where(used, peak + jnp.log(jnp.where(used, total, 1.0)), FLOOR)
        for i in range(each):
            s = each * c + i
            sl = slice(GROUP * i, GROUP * (i + 1))
            prob[s] = weights[sl].astype(BF16)
            stat_f[pl.ds(s, GROUP, stride=SLOTS), :] = jnp.broadcast_to(level[sl], (GROUP, HD))
    mine_x = rows_of(x, PAIR * SLOTS)
    st_send[...] = jnp.transpose(stat_f[...])[0:1, :]
    for dx in (2, 1, 3):
        remote(st_send, st_x.at[(NX - dx) % NX], sst, rst, at(0, dx))
    st_x[0] = st_send[...]
    c_v.wait()
    for s in range(SLOTS):
        sl = slice(GROUP * (s % each), GROUP * (s % each + 1))
        o_f[pl.ds(s, GROUP, stride=SLOTS), :] = dot(prob[s], vals[s]) * inverse[s // each][sl]
    o_send[...] = o_f[...].astype(BF16)
    for dx in (2, 1, 3):
        rows = rows_of((x + dx) % NX, PAIR * SLOTS)
        remote(o_send.at[rows], o_x.at[(NX - dx) % NX], so, ro, at(0, dx))
    o_x[0] = o_send[mine_x, :]

    arrived(st_x.at[pl.ds(1, NX - 1)], rst)
    pad = jnp.zeros((ROWS - NX, ROWS), F32)
    stat_f[...] = jnp.transpose(jnp.concatenate([st_x[e] for e in range(NX)] + [pad], axis=0))
    own = stat_f[mine_x, :]
    ws = []
    is_held = hold[...] > 0.0
    for hh in range(PAIR):
        cut = slice(hh * SLOTS, (hh + 1) * SLOTS)
        level = jnp.concatenate([own[cut, e : e + 1] for e in range(NX)], axis=0)
        top = jnp.max(jnp.where(is_held, level, FLOOR), axis=0, keepdims=True)
        w = jnp.where(is_held, jnp.exp(level - top), 0.0)
        total = jnp.sum(w, axis=0, keepdims=True)
        used = total > 0.0
        total = jnp.where(used, total, 1.0)
        w = w / total
        coarse = w.astype(BF16)
        ws.append((coarse, (w - coarse.astype(F32)).astype(BF16)))
        zst_send[hh : hh + 1, :] = jnp.where(used, top + jnp.log(total), FLOOR)
    for dz in FAR_FIRST:
        remote(zst_send, zst.at[NZ - dz], szs, rzs, at(dz, 0))
    zst[0] = zst_send[...]

    arrived(o_x.at[pl.ds(1, NX - 1)], ro)
    for hh in range(PAIR):
        data = jnp.concatenate(
            [o_x[e, hh * SLOTS : (hh + 1) * SLOTS, :] for e in range(NX)], axis=0
        )
        both = dot(ws[hh][0], data, ((0,), (0,))) + dot(ws[hh][1], data, ((0,), (0,)))
        part[:, hh * HD : (hh + 1) * HD] = both.astype(BF16)
    for dz in FAR_FIRST:
        remote(part.at[rows_of((mine + dz) % NT, BAND)], rs.at[NZ - dz], srs, rrs, at(dz, 0))
    my_band = rows_of(mine, BAND)
    rs[0] = part[my_band, :]

    arrived(wall.at[pl.ds(0, 3)], rw.at[0])
    for dt in (2, 6, 4):
        origin = (t + dt) % NT
        remote(wall.at[origin], wall.at[origin], sw.at[1], rw.at[1], sibling)

    arrived(qall.at[0, pl.ds(0, NZ - 1)], sq)
    arrived(qall.at[pl.ds(0, NX - 1)], sqx)
    arrived(wall.at[pl.ds(0, 3)], sw.at[0])
    arrived(st_x.at[pl.ds(0, NX - 1)], sst)
    arrived(o_x.at[pl.ds(0, NX - 1)], so)
    arrived(zst.at[pl.ds(0, NZ - 1)], szs)

    arrived(zst.at[pl.ds(1, NZ - 1)], rzs)
    scales = []
    for hh in range(PAIR):
        level = jnp.concatenate([zst[e, hh : hh + 1, :] for e in range(NZ)], axis=0)
        w = jnp.exp(level - jnp.max(level, axis=0, keepdims=True))
        scales.append(w / jnp.sum(w, axis=0, keepdims=True))
    pad = jnp.zeros((ROWS - PAIR * NZ, ROWS), F32)
    scale_t[...] = jnp.transpose(jnp.concatenate(scales + [pad], axis=0))
    cols = scale_t[my_band, :]
    for e in range(NZ):
        for hh in range(PAIR):
            zw[e, :, hh * HD : (hh + 1) * HD] = jnp.broadcast_to(
                cols[:, hh * NZ + e : hh * NZ + e + 1], (BAND, HD)
            )
    arrived(rs.at[pl.ds(1, NZ - 1)], rrs)
    acc = jnp.zeros((BAND, PAIR * HD), F32)
    for e in range(NZ):
        acc = acc + rs[e].astype(F32) * zw[e]
    band[...] = acc.astype(BF16)

    @pl.when(mine != t)
    def _():
        pl.semaphore_wait(seen, 1)

    reach = NZ // 2
    lowest = (z - 3 - t % 2 + NZ) % NZ
    skip = (NZ - lowest) * (lowest // (reach + 1))

    def end(step, dx):
        zz = (lowest + (step + skip) % reach) % NZ
        return zz, pltpu.make_async_remote_copy(
            src_ref=band,
            dst_ref=fin.at[(NX - dx) % NX, t],
            send_sem=sfin,
            recv_sem=rfin.at[(NX - dx) % NX],
            device_id={"pool": zz * NX + (x + dx) % NX, "tp": mine},
            device_id_type=MESH,
        )

    for step in range(reach):
        for dx in (2, 1, 3, 0):
            zz, copy = end(step, dx)
            if dx:
                copy.start()
                continue
            here = jnp.logical_and(zz == z, mine == t)

            @pl.when(jnp.logical_not(here))
            def _(copy=copy):
                copy.start()

            @pl.when(here)
            def _():
                pltpu.make_async_copy(band, fin.at[0, t], rfin.at[0]).start()

    arrived(rs.at[pl.ds(0, NZ - 1)], srs)

    c_w.wait()
    arrived(wall.at[pl.ds(0, NX)], rw.at[1])
    arrived(wall.at[pl.ds(0, NX)], sw.at[1])
    acc = jnp.zeros((BAND, HD), F32)
    for e in (0, 1, 3, 2):
        arrived(fin.at[e], rfin.at[e])
        rows = rows_of((x + e) % NX, PAIR * HD)
        for n in range(NT):
            acc = acc + dot(fin[e, n], wall[n, rows, :])
    out_ref[...] = acc.astype(BF16)
    arrived(fin.at[pl.ds(0, NX - 1)], sfin)
    arrived(fin.at[0, pl.ds(0, NT - 1)], sfin)

    @pl.when(mine != t)
    def _():
        end(0, 0)[1].wait_send()


def on_device(queries, key_cache, value_cache, out_weight, lengths, block_table):
    q = queries.reshape(2, GROUP, HD).transpose(1, 0, 2).reshape(2 * GROUP, HD)
    hbm = pl.BlockSpec(memory_space=pltpu.HBM)
    dma = pltpu.SemaphoreType.DMA
    vmem = pltpu.VMEM
    return pl.pallas_call(
        kernel,
        out_shape=pltpu.VMEM((BAND, HD), BF16),
        in_specs=[hbm] * 6,
        out_specs=pl.BlockSpec(memory_space=pltpu.VMEM),
        scratch_shapes=[
            vmem((MAXB, ROWS), jnp.int32),
            vmem((1, ROWS), jnp.int32),
            vmem((SLOTS, BLK, HD), BF16),
            vmem((SLOTS, HD, BLK), BF16),
            vmem((SLOTS, BLK, HD), BF16),
            vmem((NX, NZ, 2 * GROUP, HD), BF16),
            vmem((ROWS, ROWS * GROUP), BF16),
            vmem((ROWS, ROWS), F32),
            vmem((NX * SLOTS, ROWS), F32),
            vmem((ROWS, BLK), F32),
            vmem((SLOTS, GROUP, BLK), BF16),
            vmem((ROWS, HD), F32),
            vmem((ROWS, HD), F32),
            vmem((ROWS, HD), BF16),
            vmem((1, ROWS), F32),
            vmem((NX, 1, ROWS), F32),
            vmem((NX, PAIR * SLOTS, HD), BF16),
            vmem((PAIR, ROWS), F32),
            vmem((NZ, PAIR, ROWS), F32),
            vmem((ROWS, ROWS), F32),
            vmem((NZ, BAND, PAIR * HD), F32),
            vmem((ROWS, PAIR * HD), BF16),
            vmem((NZ, BAND, PAIR * HD), BF16),
            vmem((BAND, PAIR * HD), BF16),
            vmem((NX, NT, BAND, PAIR * HD), BF16),
            vmem((NT, GROUP * HD, HD), BF16),
            dma((6,)),
            dma,
            dma((len(LEGS),)),
            dma,
            dma,
            dma((2,)),
            dma((2,)),
            dma,
            dma,
            dma,
            dma,
            dma,
            dma,
            dma,
            dma,
            dma,
            dma((NX,)),
            pltpu.SemaphoreType.REGULAR,
        ],
        compiler_params=pltpu.CompilerParams(
            collective_id=0, has_side_effects=True, vmem_limit_bytes=56 * 1024 * 1024
        ),
        cost_estimate=pl.CostEstimate(
            flops=400_000_000, bytes_accessed=5_000_000, transcendentals=70_000
        ),
        name="lent_attention",
    )(q, key_cache, value_cache, out_weight, lengths.reshape(1, ROWS), block_table.T)


def solution(mesh):
    return jax.shard_map(
        on_device,
        mesh=mesh,
        in_specs=(
            P("pool", "tp"),
            P("tp", "pool", None, None),
            P("tp", "pool", None, None),
            P("tp", "pool"),
            P(),
            P(),
        ),
        out_specs=P("tp", "pool"),
        check_vma=False,
    )
```

```python
import functools
import math

import jax
import jax.numpy as jnp
from jax import lax
from jax.experimental import pallas as pl
from jax.experimental.pallas import tpu as pltpu
from jax.sharding import PartitionSpec as P

MESH = pl.DeviceIdType.MESH
FLOOR = -1e30
F32 = jnp.float32
BF16 = jnp.bfloat16

NZ, NX, NT = 16, 4, 8
ROWS, SLOTS, BLK, HD, GROUP, MAXB = 128, 16, 512, 128, 8, 32
PAIR = GROUP // NX
BAND = ROWS // NT
HUB = 4
ZORDER = [0, 1, 2, 3, 4, 15, 14, 13, 12, 5, 6, 7, 11, 10, 9, 8]
UP, DOWN, FAR_UP, FAR_DOWN = (1, 5), (5, 9), (9, 12), (12, 16)
NEAR = (4, 12, 3, 13, 2, 14, 1, 15)
SPREAD = 5
FAR_FIRST = (8, 7, 9, 6, 10, 5, 11, 4, 12, 3, 13, 2, 14, 1, 15)

def dot(a, b, dims=((1,), (0,))):
    return lax.dot_general(a, b, (dims, ((), ())), preferred_element_type=F32)


def kernel(
    q_hbm,
    k_hbm,
    v_hbm,
    w_hbm,
    len_hbm,
    tab_hbm,
    out_ref,
    tab,
    lens,
    keys,
    keys_t,
    vals,
    qall,
    sel,
    lims,
    hold,
    score,
    prob,
    o_f,
    stat_f,
    o_send,
    st_send,
    st_x,
    o_x,
    zst_send,
    zst,
    scale_t,
    zw,
    part,
    rs,
    band,
    fin,
    wall,
    loc_sem,
    sq,
    rq,
    sqx,
    rqx,
    sw,
    rw,
    sst,
    rst,
    so,
    ro,
    szs,
    rzs,
    srs,
    rrs,
    sfin,
    rfin,
    seen,
):
    pool = lax.axis_index("pool")
    t = lax.axis_index("tp")
    z = pool // NX
    x = pool % NX
    theirs = (z + (NT - SPREAD) * t) % NT

    def at(dz, dx):
        return {"pool": ((z + dz) % NZ) * NX + (x + dx) % NX, "tp": t}

    def finisher(dz):
        return SPREAD * (z + dz + NT - t) % NT

    def remote(src, dst, send, recv, to):
        copy = pltpu.make_async_remote_copy(
            src_ref=src,
            dst_ref=dst,
            send_sem=send,
            recv_sem=recv,
            device_id=to,
            device_id_type=MESH,
        )
        copy.start()
        return copy

    def rows_of(index, size):
        return pl.ds(pl.multiple_of(index * size, size), size)

    def arrived(ref, sem):
        pltpu.make_async_copy(ref, ref, sem).wait()

    barrier = pltpu.get_barrier_semaphore()
    for dz in NEAR:
        pl.semaphore_signal(barrier, inc=1, device_id=at(dz, 0), device_id_type=MESH)
    c_q = pltpu.make_async_copy(q_hbm, qall.at[0, 0], loc_sem.at[2])
    c_q.start()
    for dt in (4, 3, 5, 2, 6, 1, 7):
        pl.semaphore_signal(
            barrier, inc=1, device_id={"pool": pool, "tp": (t + dt) % NT}, device_id_type=MESH
        )
    for dx in (2, 1, 3):
        pl.semaphore_signal(barrier, inc=1, device_id=at(0, dx), device_id_type=MESH)
    c_tab = pltpu.make_async_copy(tab_hbm, tab, loc_sem.at[0])
    c_len = pltpu.make_async_copy(len_hbm, lens, loc_sem.at[1])
    c_k = pltpu.make_async_copy(k_hbm.at[0], keys, loc_sem.at[3])
    c_v = pltpu.make_async_copy(v_hbm.at[0], vals, loc_sem.at[4])
    c_w = pltpu.make_async_copy(w_hbm, wall.at[t], loc_sem.at[5])
    c_tab.start()
    c_len.start()
    c_k.start()
    c_v.start()
    c_w.start()
    c_q.wait()
    pl.semaphore_wait(barrier, len(NEAR) + NX - 1 + NT - 1)

    place = {dz: k for k, dz in enumerate(ZORDER)}
    for dz in NEAR:
        k = place[NZ - dz]
        remote(qall.at[0, 0], qall.at[0, k], sq, rq.at[int(k >= DOWN[0])], at(dz, 0))

    c_tab.wait()
    c_len.wait()
    tab_t = tab[...].astype(F32)
    len_row = lens[...].astype(F32)
    sub = lax.broadcasted_iota(jnp.int32, (ROWS, ROWS), 0)
    lane = lax.broadcasted_iota(jnp.int32, (ROWS, ROWS), 1)
    sid = (pool * SLOTS + sub // GROUP).astype(F32)
    left = jnp.zeros((ROWS, ROWS), F32)
    sub4 = lax.broadcasted_iota(jnp.int32, (NX * SLOTS, ROWS), 0)
    sid4 = ((z * NX + (x + sub4 // SLOTS) % NX) * SLOTS + sub4 % SLOTS).astype(F32)
    held = jnp.zeros((NX * SLOTS, ROWS), F32)
    for b in range(MAXB):
        entry = tab_t[b : b + 1, :]
        left = jnp.where(entry == sid, len_row - float(BLK * b), left)
        held = jnp.where(entry == sid4, 1.0, held)
    hold[...] = held
    lims[...] = jnp.broadcast_to(jnp.sum(left, axis=1, keepdims=True), (ROWS, ROWS))
    row_of = jnp.sum(
        jnp.where(left > 0.0, (lane + 1).astype(F32), 0.0), axis=1, keepdims=True
    )
    key_col = (row_of - 1.0) * float(GROUP) + (sub[:, 0:1] % GROUP).astype(F32)
    j = lax.broadcasted_iota(jnp.int32, (1, ROWS * GROUP), 1)
    piece = j // (2 * GROUP)
    k_j = piece % NZ
    dz_j = jnp.zeros_like(j)
    for k, dz in enumerate(ZORDER):
        dz_j = jnp.where(k_j == k, dz, dz_j)
    p_j = ((z + dz_j) % NZ) * NX + (x + piece // NZ) % NX
    key_row = ((2 * p_j + j % 2) * GROUP + (j % (2 * GROUP)) // 2).astype(F32)
    for c in range(8):
        cut = slice(c * 128, (c + 1) * 128)
        sel[:, cut] = jnp.where(key_col == key_row[:, cut], 1.0, 0.0).astype(BF16)

    def pieces(cut):
        return pl.ds(cut[0], cut[1] - cut[0])

    def across(cut):
        for dx in (2, 1, 3):
            remote(
                qall.at[0, pieces(cut)], qall.at[(NX - dx) % NX, pieces(cut)], sqx, rqx, at(0, dx)
            )

    arrived(qall.at[0, pieces(DOWN)], rq.at[1])
    remote(qall.at[0, pieces(DOWN)], qall.at[0, pieces(FAR_DOWN)], sq, rq.at[3], at(HUB, 0))
    arrived(qall.at[0, pieces(UP)], rq.at[0])
    count = pl.ds(UP[0], FAR_UP[1] - FAR_UP[0])
    remote(qall.at[0, count], qall.at[0, pieces(FAR_UP)], sq, rq.at[2], at(NZ - HUB, 0))
    across((0, DOWN[1]))
    arrived(qall.at[0, pieces(FAR_UP)], rq.at[2])
    across(FAR_UP)
    arrived(qall.at[0, pieces(FAR_DOWN)], rq.at[3])
    across(FAR_DOWN)
    sibling = {"pool": pool, "tp": t + 1 - 2 * (t % 2)}
    for dt in (2, 6, 4):
        remote(w_hbm, wall.at[t], sw.at[0], rw.at[0], {"pool": pool, "tp": (t + dt) % NT})
    remote(w_hbm, wall.at[t], sw.at[1], rw.at[1], sibling)

    c_k.wait()
    for s in range(SLOTS):
        keys_t[s] = keys[s].T
    arrived(qall.at[pl.ds(1, NX - 1)], rqx)
    for dt in (4, 3, 5, 2, 6, 1, 7):
        pl.semaphore_signal(
            seen, inc=1, device_id={"pool": pool, "tp": (t + dt) % NT}, device_id_type=MESH
        )

    picked = dot(sel[...], qall[...].reshape(ROWS * GROUP, HD))
    scaling = 1.0 / math.sqrt(HD)
    for s in range(SLOTS):
        cut = slice(GROUP * s, GROUP * (s + 1))
        score[cut] = dot(picked[cut].astype(BF16), keys_t[s])
    each = 4
    place_in = lax.broadcasted_iota(jnp.int32, (each * GROUP, BLK), 1).astype(F32)
    inverse = []
    for c in range(SLOTS // each):
        cut = slice(each * GROUP * c, each * GROUP * (c + 1))
        usable = place_in < lims[cut, 0:1]
        scores = jnp.where(usable, score[cut] * scaling, FLOOR)
        peak = jnp.max(scores, axis=1, keepdims=True)
        weights = jnp.where(usable, jnp.exp(scores - peak), 0.0)
        total = jnp.sum(weights, axis=1, keepdims=True)
        used = total > 0.0
        inverse.append(jnp.where(used, 1.0 / jnp.where(used, total, 1.0), 0.0))
        level = jnp.where(used, peak + jnp.log(jnp.where(used, total, 1.0)), FLOOR)
        for i in range(each):
            s = each * c + i
            sl = slice(GROUP * i, GROUP * (i + 1))
            prob[s] = weights[sl].astype(BF16)
            stat_f[pl.ds(s, GROUP, stride=SLOTS), :] = jnp.broadcast_to(level[sl], (GROUP, HD))
    mine_x = rows_of(x, PAIR * SLOTS)
    st_send[...] = jnp.transpose(stat_f[...])[0:1, :]
    for dx in (2, 1, 3):
        remote(st_send, st_x.at[(NX - dx) % NX], sst, rst, at(0, dx))
    st_x[0] = st_send[...]
    c_v.wait()
    for s in range(SLOTS):
        sl = slice(GROUP * (s % each), GROUP * (s % each + 1))
        o_f[pl.ds(s, GROUP, stride=SLOTS), :] = dot(prob[s], vals[s]) * inverse[s // each][sl]
    o_send[...] = o_f[...].astype(BF16)
    for dx in (2, 1, 3):
        rows = rows_of((x + dx) % NX, PAIR * SLOTS)
        remote(o_send.at[rows], o_x.at[(NX - dx) % NX], so, ro, at(0, dx))
    o_x[0] = o_send[mine_x, :]

    arrived(st_x.at[pl.ds(1, NX - 1)], rst)
    pad = jnp.zeros((ROWS - NX, ROWS), F32)
    stat_f[...] = jnp.transpose(jnp.concatenate([st_x[e] for e in range(NX)] + [pad], axis=0))
    own = stat_f[mine_x, :]
    ws = []
    is_held = hold[...] > 0.0
    for hh in range(PAIR):
        cut = slice(hh * SLOTS, (hh + 1) * SLOTS)
        level = jnp.concatenate([own[cut, e : e + 1] for e in range(NX)], axis=0)
        top = jnp.max(jnp.where(is_held, level, FLOOR), axis=0, keepdims=True)
        w = jnp.where(is_held, jnp.exp(level - top), 0.0)
        total = jnp.sum(w, axis=0, keepdims=True)
        used = total > 0.0
        total = jnp.where(used, total, 1.0)
        w = w / total
        coarse = w.astype(BF16)
        ws.append((coarse, (w - coarse.astype(F32)).astype(BF16)))
        zst_send[hh : hh + 1, :] = jnp.where(used, top + jnp.log(total), FLOOR)
    pl.semaphore_wait(seen, NT - 1)

    def hand(dz, source, target, send, recv):
        to = at(dz, 0)
        to["tp"] = finisher(dz)
        if dz:
            remote(source, target, send, recv, to)
            return

        @pl.when(finisher(0) != t)
        def _():
            remote(source, target, send, recv, to)

        @pl.when(finisher(0) == t)
        def _():
            pltpu.make_async_copy(source, target, recv).start()

    def left_here(ref, send):
        @pl.when(finisher(0) != t)
        def _():
            arrived(ref, send)

    for dz in FAR_FIRST + (0,):
        hand(dz, zst_send, zst.at[(NZ - dz) % NZ], szs, rzs)

    arrived(o_x.at[pl.ds(1, NX - 1)], ro)
    for hh in range(PAIR):
        data = jnp.concatenate(
            [o_x[e, hh * SLOTS : (hh + 1) * SLOTS, :] for e in range(NX)], axis=0
        )
        both = dot(ws[hh][0], data, ((0,), (0,))) + dot(ws[hh][1], data, ((0,), (0,)))
        part[:, hh * HD : (hh + 1) * HD] = both.astype(BF16)
    for dz in FAR_FIRST + (0,):
        hand(dz, part.at[rows_of(finisher(dz), BAND)], rs.at[(NZ - dz) % NZ], srs, rrs)
    my_band = rows_of(t, BAND)

    arrived(wall.at[pl.ds(0, 3)], rw.at[0])
    for dt in (2, 6, 4):
        origin = (t + dt) % NT
        remote(wall.at[origin], wall.at[origin], sw.at[1], rw.at[1], sibling)

    arrived(qall.at[0, pl.ds(0, NZ - 1)], sq)
    arrived(qall.at[pl.ds(0, NX - 1)], sqx)
    arrived(wall.at[pl.ds(0, 3)], sw.at[0])
    arrived(st_x.at[pl.ds(0, NX - 1)], sst)
    arrived(o_x.at[pl.ds(0, NX - 1)], so)
    arrived(zst.at[pl.ds(0, NZ - 1)], szs)
    left_here(zst.at[0], szs)

    arrived(zst, rzs)
    scales = []
    for hh in range(PAIR):
        level = jnp.concatenate([zst[e, hh : hh + 1, :] for e in range(NZ)], axis=0)
        w = jnp.exp(level - jnp.max(level, axis=0, keepdims=True))
        scales.append(w / jnp.sum(w, axis=0, keepdims=True))
    pad = jnp.zeros((ROWS - PAIR * NZ, ROWS), F32)
    scale_t[...] = jnp.transpose(jnp.concatenate(scales + [pad], axis=0))
    cols = scale_t[my_band, :]
    for e in range(NZ):
        for hh in range(PAIR):
            zw[e, :, hh * HD : (hh + 1) * HD] = jnp.broadcast_to(
                cols[:, hh * NZ + e : hh * NZ + e + 1], (BAND, HD)
            )
    arrived(rs, rrs)
    acc = jnp.zeros((BAND, PAIR * HD), F32)
    for e in range(NZ):
        acc = acc + rs[e].astype(F32) * zw[e]
    band[...] = acc.astype(BF16)

    reach = NZ // 2
    lowest = (z - 3 - t % 2 + NZ) % NZ
    skip = (NZ - lowest) * (lowest // (reach + 1))

    def end(step, dx):
        zz = (lowest + (step + skip) % reach) % NZ
        return zz, pltpu.make_async_remote_copy(
            src_ref=band,
            dst_ref=fin.at[(NX - dx) % NX, theirs],
            send_sem=sfin,
            recv_sem=rfin.at[(NX - dx) % NX],
            device_id={"pool": zz * NX + (x + dx) % NX, "tp": t},
            device_id_type=MESH,
        )

    for step in range(reach):
        for dx in (2, 1, 3, 0):
            zz, copy = end(step, dx)
            if dx:
                copy.start()
                continue

            @pl.when(zz != z)
            def _(copy=copy):
                copy.start()

    pltpu.make_async_copy(band, fin.at[0, theirs], rfin.at[0]).start()
    arrived(rs.at[pl.ds(0, NZ - 1)], srs)
    left_here(rs.at[0], srs)

    c_w.wait()
    arrived(wall.at[pl.ds(0, NX)], rw.at[1])
    arrived(wall.at[pl.ds(0, NX)], sw.at[1])
    acc = jnp.zeros((BAND, HD), F32)
    for e in (0, 1, 3, 2):
        arrived(fin.at[e], rfin.at[e])
        rows = rows_of((x + e) % NX, PAIR * HD)
        for n in range(NT):
            acc = acc + dot(fin[e, n], wall[n, rows, :])
    out_ref[...] = acc.astype(BF16)
    arrived(fin.at[pl.ds(0, NX - 1)], sfin)
    arrived(fin.at[0, pl.ds(0, NT - 1)], sfin)


def on_device(queries, key_cache, value_cache, out_weight, lengths, block_table):
    q = queries.reshape(2, GROUP, HD).transpose(1, 0, 2).reshape(2 * GROUP, HD)
    hbm = pl.BlockSpec(memory_space=pltpu.HBM)
    dma = pltpu.SemaphoreType.DMA
    vmem = pltpu.VMEM
    return pl.pallas_call(
        kernel,
        out_shape=pltpu.VMEM((BAND, HD), BF16),
        in_specs=[hbm] * 6,
        out_specs=pl.BlockSpec(memory_space=pltpu.VMEM),
        scratch_shapes=[
            vmem((MAXB, ROWS), jnp.int32),
            vmem((1, ROWS), jnp.int32),
            vmem((SLOTS, BLK, HD), BF16),
            vmem((SLOTS, HD, BLK), BF16),
            vmem((SLOTS, BLK, HD), BF16),
            vmem((NX, NZ, 2 * GROUP, HD), BF16),
            vmem((ROWS, ROWS * GROUP), BF16),
            vmem((ROWS, ROWS), F32),
            vmem((NX * SLOTS, ROWS), F32),
            vmem((ROWS, BLK), F32),
            vmem((SLOTS, GROUP, BLK), BF16),
            vmem((ROWS, HD), F32),
            vmem((ROWS, HD), F32),
            vmem((ROWS, HD), BF16),
            vmem((1, ROWS), F32),
            vmem((NX, 1, ROWS), F32),
            vmem((NX, PAIR * SLOTS, HD), BF16),
            vmem((PAIR, ROWS), F32),
            vmem((NZ, PAIR, ROWS), F32),
            vmem((ROWS, ROWS), F32),
            vmem((NZ, BAND, PAIR * HD), F32),
            vmem((ROWS, PAIR * HD), BF16),
            vmem((NZ, BAND, PAIR * HD), BF16),
            vmem((BAND, PAIR * HD), BF16),
            vmem((NX, NT, BAND, PAIR * HD), BF16),
            vmem((NT, GROUP * HD, HD), BF16),
            dma((6,)),
            dma,
            dma((4,)),
            dma,
            dma,
            dma((2,)),
            dma((2,)),
            dma,
            dma,
            dma,
            dma,
            dma,
            dma,
            dma,
            dma,
            dma,
            dma((NX,)),
            pltpu.SemaphoreType.REGULAR,
        ],
        compiler_params=pltpu.CompilerParams(
            collective_id=0, has_side_effects=True, vmem_limit_bytes=56 * 1024 * 1024
        ),
        cost_estimate=pl.CostEstimate(
            flops=400_000_000, bytes_accessed=5_000_000, transcendentals=70_000
        ),
        name="lent_attention",
    )(q, key_cache, value_cache, out_weight, lengths.reshape(1, ROWS), block_table.T)


def solution(mesh):
    return jax.shard_map(
        on_device,
        mesh=mesh,
        in_specs=(
            P("pool", "tp"),
            P("tp", "pool", None, None),
            P("tp", "pool", None, None),
            P("tp", "pool"),
            P(),
            P(),
        ),
        out_specs=P("tp", "pool"),
        check_vma=False,
    )
```

```python
import functools
import math

import jax
import jax.numpy as jnp
from jax import lax
from jax.experimental import pallas as pl
from jax.experimental.pallas import tpu as pltpu
from jax.sharding import PartitionSpec as P

MESH = pl.DeviceIdType.MESH
FLOOR = -1e30
F32 = jnp.float32
BF16 = jnp.bfloat16

NZ, NX, NT = 16, 4, 8
ROWS, SLOTS, BLK, HD, GROUP, MAXB = 128, 16, 512, 128, 8, 32
PAIR = GROUP // NX
BAND = ROWS // NT
HUB = 4
ZORDER = [0, 1, 2, 3, 4, 15, 14, 13, 12, 5, 6, 7, 11, 10, 9, 8]
UP, DOWN, FAR_UP, FAR_DOWN = (1, 5), (5, 9), (9, 12), (12, 16)
NEAR = (4, 12, 3, 13, 2, 14, 1, 15)
SPREAD = 5
FAR_FIRST = (8, 7, 9, 6, 10, 5, 11, 4, 12, 3, 13, 2, 14, 1, 15)

def dot(a, b, dims=((1,), (0,))):
    return lax.dot_general(a, b, (dims, ((), ())), preferred_element_type=F32)


def kernel(
    q_hbm,
    k_hbm,
    v_hbm,
    w_hbm,
    len_hbm,
    tab_hbm,
    out_ref,
    tab,
    lens,
    keys,
    keys_t,
    vals,
    qall,
    sel,
    lims,
    hold,
    score,
    prob,
    o_f,
    stat_f,
    o_send,
    st_send,
    st_x,
    o_x,
    zst_send,
    zst,
    scale_t,
    zw,
    part,
    rs,
    band,
    fin,
    wall,
    loc_sem,
    sq,
    rq,
    sqx,
    rqx,
    sw,
    rw,
    sst,
    rst,
    so,
    ro,
    szs,
    rzs,
    srs,
    rrs,
    sfin,
    rfin,
    seen,
):
    pool = lax.axis_index("pool")
    t = lax.axis_index("tp")
    z = pool // NX
    x = pool % NX
    theirs = (z + (NT - SPREAD) * t) % NT

    def at(dz, dx):
        return {"pool": ((z + dz) % NZ) * NX + (x + dx) % NX, "tp": t}

    def finisher(dz):
        return SPREAD * (z + dz + NT - t) % NT

    def remote(src, dst, send, recv, to):
        copy = pltpu.make_async_remote_copy(
            src_ref=src,
            dst_ref=dst,
            send_sem=send,
            recv_sem=recv,
            device_id=to,
            device_id_type=MESH,
        )
        copy.start()
        return copy

    def rows_of(index, size):
        return pl.ds(pl.multiple_of(index * size, size), size)

    def arrived(ref, sem):
        pltpu.make_async_copy(ref, ref, sem).wait()

    barrier = pltpu.get_barrier_semaphore()
    for dz in NEAR:
        pl.semaphore_signal(barrier, inc=1, device_id=at(dz, 0), device_id_type=MESH)
    c_q = pltpu.make_async_copy(q_hbm, qall.at[0, 0], loc_sem.at[2])
    c_q.start()
    for dt in (4, 3, 5, 2, 6, 1, 7):
        pl.semaphore_signal(
            barrier, inc=1, device_id={"pool": pool, "tp": (t + dt) % NT}, device_id_type=MESH
        )
    for dx in (2, 1, 3):
        pl.semaphore_signal(barrier, inc=1, device_id=at(0, dx), device_id_type=MESH)
    c_tab = pltpu.make_async_copy(tab_hbm, tab, loc_sem.at[0])
    c_len = pltpu.make_async_copy(len_hbm, lens, loc_sem.at[1])
    c_k = pltpu.make_async_copy(k_hbm.at[0], keys, loc_sem.at[3])
    c_v = pltpu.make_async_copy(v_hbm.at[0], vals, loc_sem.at[4])
    c_w = pltpu.make_async_copy(w_hbm, wall.at[t], loc_sem.at[5])
    c_tab.start()
    c_len.start()
    c_k.start()
    c_v.start()
    c_w.start()
    c_q.wait()
    pl.semaphore_wait(barrier, len(NEAR) + NX - 1 + NT - 1)

    place = {dz: k for k, dz in enumerate(ZORDER)}
    for dz in NEAR:
        k = place[NZ - dz]
        remote(qall.at[0, 0], qall.at[0, k], sq, rq.at[int(k >= DOWN[0])], at(dz, 0))

    sibling = {"pool": pool, "tp": t + 1 - 2 * (t % 2)}
    for dt in (2, 6, 4):
        remote(w_hbm, wall.at[t], sw.at[0], rw.at[0], {"pool": pool, "tp": (t + dt) % NT})
    remote(w_hbm, wall.at[t], sw.at[1], rw.at[1], sibling)

    c_tab.wait()
    c_len.wait()
    tab_t = tab[...].astype(F32)
    len_row = lens[...].astype(F32)
    sub = lax.broadcasted_iota(jnp.int32, (ROWS, ROWS), 0)
    lane = lax.broadcasted_iota(jnp.int32, (ROWS, ROWS), 1)
    sid = (pool * SLOTS + sub // GROUP).astype(F32)
    left = jnp.zeros((ROWS, ROWS), F32)
    sub4 = lax.broadcasted_iota(jnp.int32, (NX * SLOTS, ROWS), 0)
    sid4 = ((z * NX + (x + sub4 // SLOTS) % NX) * SLOTS + sub4 % SLOTS).astype(F32)
    held = jnp.zeros((NX * SLOTS, ROWS), F32)
    for b in range(MAXB):
        entry = tab_t[b : b + 1, :]
        left = jnp.where(entry == sid, len_row - float(BLK * b), left)
        held = jnp.where(entry == sid4, 1.0, held)
    hold[...] = held
    lims[...] = jnp.broadcast_to(jnp.sum(left, axis=1, keepdims=True), (ROWS, ROWS))
    row_of = jnp.sum(
        jnp.where(left > 0.0, (lane + 1).astype(F32), 0.0), axis=1, keepdims=True
    )
    key_col = (row_of - 1.0) * float(GROUP) + (sub[:, 0:1] % GROUP).astype(F32)
    j = lax.broadcasted_iota(jnp.int32, (1, ROWS * GROUP), 1)
    piece = j // (2 * GROUP)
    k_j = piece % NZ
    dz_j = jnp.zeros_like(j)
    for k, dz in enumerate(ZORDER):
        dz_j = jnp.where(k_j == k, dz, dz_j)
    p_j = ((z + dz_j) % NZ) * NX + (x + piece // NZ) % NX
    key_row = ((2 * p_j + j % 2) * GROUP + (j % (2 * GROUP)) // 2).astype(F32)
    for c in range(8):
        cut = slice(c * 128, (c + 1) * 128)
        sel[:, cut] = jnp.where(key_col == key_row[:, cut], 1.0, 0.0).astype(BF16)

    def pieces(cut):
        return pl.ds(cut[0], cut[1] - cut[0])

    def across(cut):
        for dx in (2, 1, 3):
            remote(
                qall.at[0, pieces(cut)], qall.at[(NX - dx) % NX, pieces(cut)], sqx, rqx, at(0, dx)
            )

    arrived(qall.at[0, pieces(DOWN)], rq.at[1])
    remote(qall.at[0, pieces(DOWN)], qall.at[0, pieces(FAR_DOWN)], sq, rq.at[3], at(HUB, 0))
    arrived(qall.at[0, pieces(UP)], rq.at[0])
    count = pl.ds(UP[0], FAR_UP[1] - FAR_UP[0])
    remote(qall.at[0, count], qall.at[0, pieces(FAR_UP)], sq, rq.at[2], at(NZ - HUB, 0))
    across((0, DOWN[1]))
    arrived(qall.at[0, pieces(FAR_UP)], rq.at[2])
    across(FAR_UP)
    arrived(qall.at[0, pieces(FAR_DOWN)], rq.at[3])
    across(FAR_DOWN)
    c_k.wait()
    for s in range(SLOTS):
        keys_t[s] = keys[s].T
    arrived(qall.at[pl.ds(1, NX - 1)], rqx)
    for dt in (4, 3, 5, 2, 6, 1, 7):
        pl.semaphore_signal(
            seen, inc=1, device_id={"pool": pool, "tp": (t + dt) % NT}, device_id_type=MESH
        )

    picked = dot(sel[...], qall[...].reshape(ROWS * GROUP, HD))
    scaling = 1.0 / math.sqrt(HD)
    for s in range(SLOTS):
        cut = slice(GROUP * s, GROUP * (s + 1))
        score[cut] = dot(picked[cut].astype(BF16), keys_t[s])
    each = 4
    place_in = lax.broadcasted_iota(jnp.int32, (each * GROUP, BLK), 1).astype(F32)
    inverse = []
    for c in range(SLOTS // each):
        cut = slice(each * GROUP * c, each * GROUP * (c + 1))
        usable = place_in < lims[cut, 0:1]
        scores = jnp.where(usable, score[cut] * scaling, FLOOR)
        peak = jnp.max(scores, axis=1, keepdims=True)
        weights = jnp.where(usable, jnp.exp(scores - peak), 0.0)
        total = jnp.sum(weights, axis=1, keepdims=True)
        used = total > 0.0
        inverse.append(jnp.where(used, 1.0 / jnp.where(used, total, 1.0), 0.0))
        level = jnp.where(used, peak + jnp.log(jnp.where(used, total, 1.0)), FLOOR)
        for i in range(each):
            s = each * c + i
            sl = slice(GROUP * i, GROUP * (i + 1))
            prob[s] = weights[sl].astype(BF16)
            stat_f[pl.ds(s, GROUP, stride=SLOTS), :] = jnp.broadcast_to(level[sl], (GROUP, HD))
    mine_x = rows_of(x, PAIR * SLOTS)
    st_send[...] = jnp.transpose(stat_f[...])[0:1, :]
    for dx in (2, 1, 3):
        remote(st_send, st_x.at[(NX - dx) % NX], sst, rst, at(0, dx))
    st_x[0] = st_send[...]
    c_v.wait()
    for s in range(SLOTS):
        sl = slice(GROUP * (s % each), GROUP * (s % each + 1))
        o_f[pl.ds(s, GROUP, stride=SLOTS), :] = dot(prob[s], vals[s]) * inverse[s // each][sl]
    o_send[...] = o_f[...].astype(BF16)
    for dx in (2, 1, 3):
        rows = rows_of((x + dx) % NX, PAIR * SLOTS)
        remote(o_send.at[rows], o_x.at[(NX - dx) % NX], so, ro, at(0, dx))
    o_x[0] = o_send[mine_x, :]

    arrived(st_x.at[pl.ds(1, NX - 1)], rst)
    pad = jnp.zeros((ROWS - NX, ROWS), F32)
    stat_f[...] = jnp.transpose(jnp.concatenate([st_x[e] for e in range(NX)] + [pad], axis=0))
    own = stat_f[mine_x, :]
    ws = []
    is_held = hold[...] > 0.0
    for hh in range(PAIR):
        cut = slice(hh * SLOTS, (hh + 1) * SLOTS)
        level = jnp.concatenate([own[cut, e : e + 1] for e in range(NX)], axis=0)
        top = jnp.max(jnp.where(is_held, level, FLOOR), axis=0, keepdims=True)
        w = jnp.where(is_held, jnp.exp(level - top), 0.0)
        total = jnp.sum(w, axis=0, keepdims=True)
        used = total > 0.0
        total = jnp.where(used, total, 1.0)
        w = w / total
        coarse = w.astype(BF16)
        ws.append((coarse, (w - coarse.astype(F32)).astype(BF16)))
        zst_send[hh : hh + 1, :] = jnp.where(used, top + jnp.log(total), FLOOR)
    pl.semaphore_wait(seen, NT - 1)

    def hand(dz, source, target, send, recv):
        to = at(dz, 0)
        to["tp"] = finisher(dz)
        if dz:
            remote(source, target, send, recv, to)
            return

        @pl.when(finisher(0) != t)
        def _():
            remote(source, target, send, recv, to)

        @pl.when(finisher(0) == t)
        def _():
            pltpu.make_async_copy(source, target, recv).start()

    def left_here(ref, send):
        @pl.when(finisher(0) != t)
        def _():
            arrived(ref, send)

    for dz in FAR_FIRST + (0,):
        hand(dz, zst_send, zst.at[(NZ - dz) % NZ], szs, rzs)

    arrived(o_x.at[pl.ds(1, NX - 1)], ro)
    for hh in range(PAIR):
        data = jnp.concatenate(
            [o_x[e, hh * SLOTS : (hh + 1) * SLOTS, :] for e in range(NX)], axis=0
        )
        both = dot(ws[hh][0], data, ((0,), (0,))) + dot(ws[hh][1], data, ((0,), (0,)))
        part[:, hh * HD : (hh + 1) * HD] = both.astype(BF16)
    for dz in FAR_FIRST + (0,):
        hand(dz, part.at[rows_of(finisher(dz), BAND)], rs.at[(NZ - dz) % NZ], srs, rrs)
    my_band = rows_of(t, BAND)

    arrived(wall.at[pl.ds(0, 3)], rw.at[0])
    for dt in (2, 6, 4):
        origin = (t + dt) % NT
        remote(wall.at[origin], wall.at[origin], sw.at[1], rw.at[1], sibling)

    arrived(qall.at[0, pl.ds(0, NZ - 1)], sq)
    arrived(qall.at[pl.ds(0, NX - 1)], sqx)
    arrived(wall.at[pl.ds(0, 3)], sw.at[0])
    arrived(st_x.at[pl.ds(0, NX - 1)], sst)
    arrived(o_x.at[pl.ds(0, NX - 1)], so)
    arrived(zst.at[pl.ds(0, NZ - 1)], szs)
    left_here(zst.at[0], szs)

    arrived(zst, rzs)
    scales = []
    for hh in range(PAIR):
        level = jnp.concatenate([zst[e, hh : hh + 1, :] for e in range(NZ)], axis=0)
        w = jnp.exp(level - jnp.max(level, axis=0, keepdims=True))
        scales.append(w / jnp.sum(w, axis=0, keepdims=True))
    pad = jnp.zeros((ROWS - PAIR * NZ, ROWS), F32)
    scale_t[...] = jnp.transpose(jnp.concatenate(scales + [pad], axis=0))
    cols = scale_t[my_band, :]
    for e in range(NZ):
        for hh in range(PAIR):
            zw[e, :, hh * HD : (hh + 1) * HD] = jnp.broadcast_to(
                cols[:, hh * NZ + e : hh * NZ + e + 1], (BAND, HD)
            )
    arrived(rs, rrs)
    acc = jnp.zeros((BAND, PAIR * HD), F32)
    for e in range(NZ):
        acc = acc + rs[e].astype(F32) * zw[e]
    band[...] = acc.astype(BF16)

    reach = NZ // 2
    lowest = (z - 3 - t % 2 + NZ) % NZ
    skip = (NZ - lowest) * (lowest // (reach + 1))

    def end(step, dx):
        zz = (lowest + (step + skip) % reach) % NZ
        return zz, pltpu.make_async_remote_copy(
            src_ref=band,
            dst_ref=fin.at[(NX - dx) % NX, theirs],
            send_sem=sfin,
            recv_sem=rfin.at[(NX - dx) % NX],
            device_id={"pool": zz * NX + (x + dx) % NX, "tp": t},
            device_id_type=MESH,
        )

    for step in range(reach):
        for dx in (2, 1, 3, 0):
            zz, copy = end(step, dx)
            if dx:
                copy.start()
                continue

            @pl.when(zz != z)
            def _(copy=copy):
                copy.start()

    pltpu.make_async_copy(band, fin.at[0, theirs], rfin.at[0]).start()
    arrived(rs.at[pl.ds(0, NZ - 1)], srs)
    left_here(rs.at[0], srs)

    c_w.wait()
    arrived(wall.at[pl.ds(0, NX)], rw.at[1])
    arrived(wall.at[pl.ds(0, NX)], sw.at[1])
    acc = jnp.zeros((BAND, HD), F32)
    for e in (0, 1, 3, 2):
        arrived(fin.at[e], rfin.at[e])
        rows = rows_of((x + e) % NX, PAIR * HD)
        for n in range(NT):
            acc = acc + dot(fin[e, n], wall[n, rows, :])
    out_ref[...] = acc.astype(BF16)
    arrived(fin.at[pl.ds(0, NX - 1)], sfin)
    arrived(fin.at[0, pl.ds(0, NT - 1)], sfin)


def on_device(queries, key_cache, value_cache, out_weight, lengths, block_table):
    q = queries.reshape(2, GROUP, HD).transpose(1, 0, 2).reshape(2 * GROUP, HD)
    hbm = pl.BlockSpec(memory_space=pltpu.HBM)
    dma = pltpu.SemaphoreType.DMA
    vmem = pltpu.VMEM
    return pl.pallas_call(
        kernel,
        out_shape=pltpu.VMEM((BAND, HD), BF16),
        in_specs=[hbm] * 6,
        out_specs=pl.BlockSpec(memory_space=pltpu.VMEM),
        scratch_shapes=[
            vmem((MAXB, ROWS), jnp.int32),
            vmem((1, ROWS), jnp.int32),
            vmem((SLOTS, BLK, HD), BF16),
            vmem((SLOTS, HD, BLK), BF16),
            vmem((SLOTS, BLK, HD), BF16),
            vmem((NX, NZ, 2 * GROUP, HD), BF16),
            vmem((ROWS, ROWS * GROUP), BF16),
            vmem((ROWS, ROWS), F32),
            vmem((NX * SLOTS, ROWS), F32),
            vmem((ROWS, BLK), F32),
            vmem((SLOTS, GROUP, BLK), BF16),
            vmem((ROWS, HD), F32),
            vmem((ROWS, HD), F32),
            vmem((ROWS, HD), BF16),
            vmem((1, ROWS), F32),
            vmem((NX, 1, ROWS), F32),
            vmem((NX, PAIR * SLOTS, HD), BF16),
            vmem((PAIR, ROWS), F32),
            vmem((NZ, PAIR, ROWS), F32),
            vmem((ROWS, ROWS), F32),
            vmem((NZ, BAND, PAIR * HD), F32),
            vmem((ROWS, PAIR * HD), BF16),
            vmem((NZ, BAND, PAIR * HD), BF16),
            vmem((BAND, PAIR * HD), BF16),
            vmem((NX, NT, BAND, PAIR * HD), BF16),
            vmem((NT, GROUP * HD, HD), BF16),
            dma((6,)),
            dma,
            dma((4,)),
            dma,
            dma,
            dma((2,)),
            dma((2,)),
            dma,
            dma,
            dma,
            dma,
            dma,
            dma,
            dma,
            dma,
            dma,
            dma((NX,)),
            pltpu.SemaphoreType.REGULAR,
        ],
        compiler_params=pltpu.CompilerParams(
            collective_id=0, has_side_effects=True, vmem_limit_bytes=56 * 1024 * 1024
        ),
        cost_estimate=pl.CostEstimate(
            flops=400_000_000, bytes_accessed=5_000_000, transcendentals=70_000
        ),
        name="lent_attention",
    )(q, key_cache, value_cache, out_weight, lengths.reshape(1, ROWS), block_table.T)


def solution(mesh):
    return jax.shard_map(
        on_device,
        mesh=mesh,
        in_specs=(
            P("pool", "tp"),
            P("tp", "pool", None, None),
            P("tp", "pool", None, None),
            P("tp", "pool"),
            P(),
            P(),
        ),
        out_specs=P("tp", "pool"),
        check_vma=False,
    )
```

```python
import functools
import math

import jax
import jax.numpy as jnp
from jax import lax
from jax.experimental import pallas as pl
from jax.experimental.pallas import tpu as pltpu
from jax.sharding import PartitionSpec as P

MESH = pl.DeviceIdType.MESH
FLOOR = -1e30
F32 = jnp.float32
BF16 = jnp.bfloat16

NZ, NX, NT = 16, 4, 8
ROWS, SLOTS, BLK, HD, GROUP, MAXB = 128, 16, 512, 128, 8, 32
PAIR = GROUP // NX
BAND = ROWS // NT
HUB = 4
ZORDER = [0, 1, 2, 3, 4, 15, 14, 13, 12, 5, 6, 7, 11, 10, 9, 8]
UP, DOWN, FAR_UP, FAR_DOWN = (1, 5), (5, 9), (9, 12), (12, 16)
NEAR = (4, 12, 3, 13, 2, 14, 1, 15)
SPREAD = 5
FAR_FIRST = (8, 7, 9, 6, 10, 5, 11, 4, 12, 3, 13, 2, 14, 1, 15)

def dot(a, b, dims=((1,), (0,))):
    return lax.dot_general(a, b, (dims, ((), ())), preferred_element_type=F32)


def kernel(
    q_hbm,
    k_hbm,
    v_hbm,
    w_hbm,
    len_hbm,
    tab_hbm,
    out_ref,
    tab,
    lens,
    keys,
    keys_t,
    vals,
    qall,
    sel,
    lims,
    hold,
    score,
    prob,
    o_f,
    o_send,
    st_send,
    st_x,
    o_x,
    zst_send,
    zst,
    scale_t,
    zw,
    part,
    rs,
    band,
    fin,
    wall,
    loc_sem,
    sq,
    rq,
    sqx,
    rqx,
    sw,
    rw,
    sst,
    rst,
    so,
    ro,
    szs,
    rzs,
    srs,
    rrs,
    sfin,
    rfin,
    seen,
):
    pool = lax.axis_index("pool")
    t = lax.axis_index("tp")
    z = pool // NX
    x = pool % NX
    theirs = (z + (NT - SPREAD) * t) % NT

    def at(dz, dx):
        return {"pool": ((z + dz) % NZ) * NX + (x + dx) % NX, "tp": t}

    def finisher(dz):
        return SPREAD * (z + dz + NT - t) % NT

    def remote(src, dst, send, recv, to):
        copy = pltpu.make_async_remote_copy(
            src_ref=src,
            dst_ref=dst,
            send_sem=send,
            recv_sem=recv,
            device_id=to,
            device_id_type=MESH,
        )
        copy.start()
        return copy

    def rows_of(index, size):
        return pl.ds(pl.multiple_of(index * size, size), size)

    def arrived(ref, sem):
        pltpu.make_async_copy(ref, ref, sem).wait()

    barrier = pltpu.get_barrier_semaphore()
    for dz in NEAR:
        pl.semaphore_signal(barrier, inc=1, device_id=at(dz, 0), device_id_type=MESH)
    c_q = pltpu.make_async_copy(q_hbm, qall.at[0, 0], loc_sem.at[2])
    c_q.start()
    for dt in (4, 3, 5, 2, 6, 1, 7):
        pl.semaphore_signal(
            barrier, inc=1, device_id={"pool": pool, "tp": (t + dt) % NT}, device_id_type=MESH
        )
    for dx in (2, 1, 3):
        pl.semaphore_signal(barrier, inc=1, device_id=at(0, dx), device_id_type=MESH)
    c_tab = pltpu.make_async_copy(tab_hbm, tab, loc_sem.at[0])
    c_len = pltpu.make_async_copy(len_hbm, lens, loc_sem.at[1])
    c_k = pltpu.make_async_copy(k_hbm.at[0], keys, loc_sem.at[3])
    c_v = pltpu.make_async_copy(v_hbm.at[0], vals, loc_sem.at[4])
    c_w = pltpu.make_async_copy(w_hbm, wall.at[t], loc_sem.at[5])
    c_tab.start()
    c_len.start()
    c_k.start()
    c_v.start()
    c_w.start()
    c_q.wait()
    pl.semaphore_wait(barrier, len(NEAR) + NX - 1 + NT - 1)

    place = {dz: k for k, dz in enumerate(ZORDER)}
    for dz in NEAR:
        k = place[NZ - dz]
        remote(qall.at[0, 0], qall.at[0, k], sq, rq.at[int(k >= DOWN[0])], at(dz, 0))

    sibling = {"pool": pool, "tp": t + 1 - 2 * (t % 2)}
    for dt in (2, 6, 4):
        remote(w_hbm, wall.at[t], sw.at[0], rw.at[0], {"pool": pool, "tp": (t + dt) % NT})
    remote(w_hbm, wall.at[t], sw.at[1], rw.at[1], sibling)

    c_tab.wait()
    c_len.wait()
    tab_t = tab[...].astype(F32)
    len_row = lens[...].astype(F32)
    sub = lax.broadcasted_iota(jnp.int32, (ROWS, ROWS), 0)
    lane = lax.broadcasted_iota(jnp.int32, (ROWS, ROWS), 1)
    sid = (pool * SLOTS + sub // GROUP).astype(F32)
    left = jnp.zeros((ROWS, ROWS), F32)
    sub4 = lax.broadcasted_iota(jnp.int32, (NX * SLOTS, ROWS), 0)
    sid4 = ((z * NX + (x + sub4 // SLOTS) % NX) * SLOTS + sub4 % SLOTS).astype(F32)
    held = jnp.zeros((NX * SLOTS, ROWS), F32)
    for b in range(MAXB):
        entry = tab_t[b : b + 1, :]
        left = jnp.where(entry == sid, len_row - float(BLK * b), left)
        held = jnp.where(entry == sid4, 1.0, held)
    hold[...] = held
    lims[...] = jnp.broadcast_to(jnp.sum(left, axis=1, keepdims=True), (ROWS, ROWS))
    row_of = jnp.sum(
        jnp.where(left > 0.0, (lane + 1).astype(F32), 0.0), axis=1, keepdims=True
    )
    key_col = (row_of - 1.0) * float(GROUP) + (sub[:, 0:1] % GROUP).astype(F32)
    j = lax.broadcasted_iota(jnp.int32, (1, ROWS * GROUP), 1)
    piece = j // (2 * GROUP)
    k_j = piece % NZ
    dz_j = jnp.zeros_like(j)
    for k, dz in enumerate(ZORDER):
        dz_j = jnp.where(k_j == k, dz, dz_j)
    p_j = ((z + dz_j) % NZ) * NX + (x + piece // NZ) % NX
    key_row = ((2 * p_j + j % 2) * GROUP + (j % (2 * GROUP)) // 2).astype(F32)
    for c in range(8):
        cut = slice(c * 128, (c + 1) * 128)
        sel[:, cut] = jnp.where(key_col == key_row[:, cut], 1.0, 0.0).astype(BF16)

    def pieces(cut):
        return pl.ds(cut[0], cut[1] - cut[0])

    def across(cut):
        for dx in (2, 1, 3):
            remote(
                qall.at[0, pieces(cut)], qall.at[(NX - dx) % NX, pieces(cut)], sqx, rqx, at(0, dx)
            )

    arrived(qall.at[0, pieces(DOWN)], rq.at[1])
    remote(qall.at[0, pieces(DOWN)], qall.at[0, pieces(FAR_DOWN)], sq, rq.at[3], at(HUB, 0))
    arrived(qall.at[0, pieces(UP)], rq.at[0])
    count = pl.ds(UP[0], FAR_UP[1] - FAR_UP[0])
    remote(qall.at[0, count], qall.at[0, pieces(FAR_UP)], sq, rq.at[2], at(NZ - HUB, 0))
    across((0, DOWN[1]))
    arrived(qall.at[0, pieces(FAR_UP)], rq.at[2])
    across(FAR_UP)
    arrived(qall.at[0, pieces(FAR_DOWN)], rq.at[3])
    across(FAR_DOWN)
    c_k.wait()
    for s in range(SLOTS):
        keys_t[s] = keys[s].T
    arrived(qall.at[pl.ds(1, NX - 1)], rqx)
    for dt in (4, 3, 5, 2, 6, 1, 7):
        pl.semaphore_signal(
            seen, inc=1, device_id={"pool": pool, "tp": (t + dt) % NT}, device_id_type=MESH
        )

    picked = dot(sel[...], qall[...].reshape(ROWS * GROUP, HD))
    scaling = 1.0 / math.sqrt(HD)
    for s in range(SLOTS):
        cut = slice(GROUP * s, GROUP * (s + 1))
        score[cut] = dot(picked[cut].astype(BF16), keys_t[s])
    each = 4
    place_in = lax.broadcasted_iota(jnp.int32, (each * GROUP, BLK), 1).astype(F32)
    inverse = []
    spot = sub % GROUP * SLOTS + sub // GROUP
    levels = jnp.zeros((1, ROWS), F32)
    for c in range(SLOTS // each):
        cut = slice(each * GROUP * c, each * GROUP * (c + 1))
        usable = place_in < lims[cut, 0:1]
        scores = jnp.where(usable, score[cut] * scaling, FLOOR)
        peak = jnp.max(scores, axis=1, keepdims=True)
        weights = jnp.where(usable, jnp.exp(scores - peak), 0.0)
        total = jnp.sum(weights, axis=1, keepdims=True)
        used = total > 0.0
        inverse.append(jnp.where(used, 1.0 / jnp.where(used, total, 1.0), 0.0))
        level = jnp.where(used, peak + jnp.log(jnp.where(used, total, 1.0)), FLOOR)
        levels = levels + jnp.sum(
            jnp.where(lane[cut] == spot[cut], level, 0.0), axis=0, keepdims=True
        )
        for i in range(each):
            s = each * c + i
            sl = slice(GROUP * i, GROUP * (i + 1))
            prob[s] = weights[sl].astype(BF16)
    mine_x = rows_of(x, PAIR * SLOTS)
    st_send[...] = levels
    for dx in (2, 1, 3):
        remote(st_send, st_x.at[(NX - dx) % NX], sst, rst, at(0, dx))
    st_x[0] = st_send[...]
    c_v.wait()
    for s in range(SLOTS):
        sl = slice(GROUP * (s % each), GROUP * (s % each + 1))
        o_f[pl.ds(s, GROUP, stride=SLOTS), :] = dot(prob[s], vals[s]) * inverse[s // each][sl]
    o_send[...] = o_f[...].astype(BF16)
    for dx in (2, 1, 3):
        rows = rows_of((x + dx) % NX, PAIR * SLOTS)
        remote(o_send.at[rows], o_x.at[(NX - dx) % NX], so, ro, at(0, dx))
    o_x[0] = o_send[mine_x, :]

    arrived(st_x.at[pl.ds(1, NX - 1)], rst)
    every = jnp.concatenate(
        [jnp.broadcast_to(st_x[e], (SLOTS, ROWS)) for e in range(NX)], axis=0
    )
    lane4 = lax.broadcasted_iota(jnp.int32, (NX * SLOTS, ROWS), 1)
    ws = []
    is_held = hold[...] > 0.0
    for hh in range(PAIR):
        mine = lane4 == (x * PAIR + hh) * SLOTS + sub4 % SLOTS
        level = jnp.sum(jnp.where(mine, every, 0.0), axis=1, keepdims=True)
        top = jnp.max(jnp.where(is_held, level, FLOOR), axis=0, keepdims=True)
        w = jnp.where(is_held, jnp.exp(level - top), 0.0)
        total = jnp.sum(w, axis=0, keepdims=True)
        used = total > 0.0
        total = jnp.where(used, total, 1.0)
        w = w / total
        coarse = w.astype(BF16)
        ws.append((coarse, (w - coarse.astype(F32)).astype(BF16)))
        zst_send[hh : hh + 1, :] = jnp.where(used, top + jnp.log(total), FLOOR)
    pl.semaphore_wait(seen, NT - 1)

    def hand(dz, source, target, send, recv):
        to = at(dz, 0)
        to["tp"] = finisher(dz)
        if dz:
            remote(source, target, send, recv, to)
            return

        @pl.when(finisher(0) != t)
        def _():
            remote(source, target, send, recv, to)

        @pl.when(finisher(0) == t)
        def _():
            pltpu.make_async_copy(source, target, recv).start()

    def left_here(ref, send):
        @pl.when(finisher(0) != t)
        def _():
            arrived(ref, send)

    for dz in FAR_FIRST + (0,):
        hand(dz, zst_send, zst.at[(NZ - dz) % NZ], szs, rzs)

    arrived(o_x.at[pl.ds(1, NX - 1)], ro)
    for hh in range(PAIR):
        data = jnp.concatenate(
            [o_x[e, hh * SLOTS : (hh + 1) * SLOTS, :] for e in range(NX)], axis=0
        )
        both = dot(ws[hh][0], data, ((0,), (0,))) + dot(ws[hh][1], data, ((0,), (0,)))
        part[:, hh * HD : (hh + 1) * HD] = both.astype(BF16)
    for dz in FAR_FIRST + (0,):
        hand(dz, part.at[rows_of(finisher(dz), BAND)], rs.at[(NZ - dz) % NZ], srs, rrs)
    my_band = rows_of(t, BAND)

    arrived(wall.at[pl.ds(0, 3)], rw.at[0])
    for dt in (2, 6, 4):
        origin = (t + dt) % NT
        remote(wall.at[origin], wall.at[origin], sw.at[1], rw.at[1], sibling)

    arrived(qall.at[0, pl.ds(0, NZ - 1)], sq)
    arrived(qall.at[pl.ds(0, NX - 1)], sqx)
    arrived(wall.at[pl.ds(0, 3)], sw.at[0])
    arrived(st_x.at[pl.ds(0, NX - 1)], sst)
    arrived(o_x.at[pl.ds(0, NX - 1)], so)
    arrived(zst.at[pl.ds(0, NZ - 1)], szs)
    left_here(zst.at[0], szs)

    arrived(zst, rzs)
    scales = []
    for hh in range(PAIR):
        level = jnp.concatenate([zst[e, hh : hh + 1, :] for e in range(NZ)], axis=0)
        w = jnp.exp(level - jnp.max(level, axis=0, keepdims=True))
        scales.append(w / jnp.sum(w, axis=0, keepdims=True))
    pad = jnp.zeros((ROWS - PAIR * NZ, ROWS), F32)
    scale_t[...] = jnp.transpose(jnp.concatenate(scales + [pad], axis=0))
    cols = scale_t[my_band, :]
    for e in range(NZ):
        for hh in range(PAIR):
            zw[e, :, hh * HD : (hh + 1) * HD] = jnp.broadcast_to(
                cols[:, hh * NZ + e : hh * NZ + e + 1], (BAND, HD)
            )
    arrived(rs, rrs)
    acc = jnp.zeros((BAND, PAIR * HD), F32)
    for e in range(NZ):
        acc = acc + rs[e].astype(F32) * zw[e]
    band[...] = acc.astype(BF16)

    reach = NZ // 2
    lowest = (z - 4 + t % 2 + NZ) % NZ
    skip = (NZ - lowest) * (lowest // (reach + 1))

    def end(step, dx):
        zz = (lowest + (step + skip) % reach) % NZ
        return zz, pltpu.make_async_remote_copy(
            src_ref=band,
            dst_ref=fin.at[(NX - dx) % NX, theirs],
            send_sem=sfin,
            recv_sem=rfin.at[(NX - dx) % NX],
            device_id={"pool": zz * NX + (x + dx) % NX, "tp": t},
            device_id_type=MESH,
        )

    for step in range(reach):
        for dx in (2, 1, 3, 0):
            zz, copy = end(step, dx)
            if dx:
                copy.start()
                continue

            @pl.when(zz != z)
            def _(copy=copy):
                copy.start()

    pltpu.make_async_copy(band, fin.at[0, theirs], rfin.at[0]).start()
    arrived(rs.at[pl.ds(0, NZ - 1)], srs)
    left_here(rs.at[0], srs)

    c_w.wait()
    arrived(wall.at[pl.ds(0, NX)], rw.at[1])
    arrived(wall.at[pl.ds(0, NX)], sw.at[1])
    acc = jnp.zeros((BAND, HD), F32)
    for e in (0, 1, 3, 2):
        arrived(fin.at[e], rfin.at[e])
        rows = rows_of((x + e) % NX, PAIR * HD)
        for n in range(NT):
            acc = acc + dot(fin[e, n], wall[n, rows, :])
    out_ref[...] = acc.astype(BF16)
    arrived(fin.at[pl.ds(0, NX - 1)], sfin)
    arrived(fin.at[0, pl.ds(0, NT - 1)], sfin)


def on_device(queries, key_cache, value_cache, out_weight, lengths, block_table):
    q = queries.reshape(2, GROUP, HD).transpose(1, 0, 2).reshape(2 * GROUP, HD)
    hbm = pl.BlockSpec(memory_space=pltpu.HBM)
    dma = pltpu.SemaphoreType.DMA
    vmem = pltpu.VMEM
    return pl.pallas_call(
        kernel,
        out_shape=pltpu.VMEM((BAND, HD), BF16),
        in_specs=[hbm] * 6,
        out_specs=pl.BlockSpec(memory_space=pltpu.VMEM),
        scratch_shapes=[
            vmem((MAXB, ROWS), jnp.int32),
            vmem((1, ROWS), jnp.int32),
            vmem((SLOTS, BLK, HD), BF16),
            vmem((SLOTS, HD, BLK), BF16),
            vmem((SLOTS, BLK, HD), BF16),
            vmem((NX, NZ, 2 * GROUP, HD), BF16),
            vmem((ROWS, ROWS * GROUP), BF16),
            vmem((ROWS, ROWS), F32),
            vmem((NX * SLOTS, ROWS), F32),
            vmem((ROWS, BLK), F32),
            vmem((SLOTS, GROUP, BLK), BF16),
            vmem((ROWS, HD), F32),
            vmem((ROWS, HD), BF16),
            vmem((1, ROWS), F32),
            vmem((NX, 1, ROWS), F32),
            vmem((NX, PAIR * SLOTS, HD), BF16),
            vmem((PAIR, ROWS), F32),
            vmem((NZ, PAIR, ROWS), F32),
            vmem((ROWS, ROWS), F32),
            vmem((NZ, BAND, PAIR * HD), F32),
            vmem((ROWS, PAIR * HD), BF16),
            vmem((NZ, BAND, PAIR * HD), BF16),
            vmem((BAND, PAIR * HD), BF16),
            vmem((NX, NT, BAND, PAIR * HD), BF16),
            vmem((NT, GROUP * HD, HD), BF16),
            dma((6,)),
            dma,
            dma((4,)),
            dma,
            dma,
            dma((2,)),
            dma((2,)),
            dma,
            dma,
            dma,
            dma,
            dma,
            dma,
            dma,
            dma,
            dma,
            dma((NX,)),
            pltpu.SemaphoreType.REGULAR,
        ],
        compiler_params=pltpu.CompilerParams(
            collective_id=0, has_side_effects=True, vmem_limit_bytes=56 * 1024 * 1024
        ),
        cost_estimate=pl.CostEstimate(
            flops=400_000_000, bytes_accessed=5_000_000, transcendentals=70_000
        ),
        name="lent_attention",
    )(q, key_cache, value_cache, out_weight, lengths.reshape(1, ROWS), block_table.T)


def solution(mesh):
    return jax.shard_map(
        on_device,
        mesh=mesh,
        in_specs=(
            P("pool", "tp"),
            P("tp", "pool", None, None),
            P("tp", "pool", None, None),
            P("tp", "pool"),
            P(),
            P(),
        ),
        out_specs=P("tp", "pool"),
        check_vma=False,
    )
```

```python
import functools
import math

import jax
import jax.numpy as jnp
from jax import lax
from jax.experimental import pallas as pl
from jax.experimental.pallas import tpu as pltpu
from jax.sharding import PartitionSpec as P

MESH = pl.DeviceIdType.MESH
FLOOR = -1e30
F32 = jnp.float32
BF16 = jnp.bfloat16

NZ, NX, NT = 16, 4, 8
ROWS, SLOTS, BLK, HD, GROUP, MAXB = 128, 16, 512, 128, 8, 32
PAIR = GROUP // NX
BAND = ROWS // NT
HUB = 4
ZORDER = [0, 1, 2, 3, 4, 15, 14, 13, 12, 5, 6, 7, 11, 10, 9, 8]
UP, DOWN, FAR_UP, FAR_DOWN = (1, 5), (5, 9), (9, 12), (12, 16)
NEAR = (4, 12, 3, 13, 2, 14, 1, 15)
SPREAD = 5
FAR_FIRST = (8, 7, 9, 6, 10, 5, 11, 4, 12, 3, 13, 2, 14, 1, 15)

def dot(a, b, dims=((1,), (0,))):
    return lax.dot_general(a, b, (dims, ((), ())), preferred_element_type=F32)


def kernel(
    q_hbm,
    k_hbm,
    v_hbm,
    w_hbm,
    len_hbm,
    tab_hbm,
    out_ref,
    tab,
    lens,
    keys,
    keys_t,
    vals,
    qall,
    sel,
    lims,
    hold,
    score,
    prob,
    o_f,
    o_send,
    st_send,
    st_x,
    o_x,
    zst_send,
    zst,
    scale_t,
    zw,
    part,
    rs,
    band,
    fin,
    wall,
    loc_sem,
    sq,
    rq,
    sqx,
    rqx,
    sw,
    rw,
    sst,
    rst,
    so,
    ro,
    szs,
    rzs,
    srs,
    rrs,
    sfin,
    rfin,
    seen,
):
    pool = lax.axis_index("pool")
    t = lax.axis_index("tp")
    z = pool // NX
    x = pool % NX
    theirs = (z + (NT - SPREAD) * t) % NT

    def at(dz, dx):
        return {"pool": ((z + dz) % NZ) * NX + (x + dx) % NX, "tp": t}

    def finisher(dz):
        return SPREAD * (z + dz + NT - t) % NT

    def remote(src, dst, send, recv, to):
        copy = pltpu.make_async_remote_copy(
            src_ref=src,
            dst_ref=dst,
            send_sem=send,
            recv_sem=recv,
            device_id=to,
            device_id_type=MESH,
        )
        copy.start()
        return copy

    def rows_of(index, size):
        return pl.ds(pl.multiple_of(index * size, size), size)

    def arrived(ref, sem):
        pltpu.make_async_copy(ref, ref, sem).wait()

    barrier = pltpu.get_barrier_semaphore()
    for dz in NEAR:
        pl.semaphore_signal(barrier, inc=1, device_id=at(dz, 0), device_id_type=MESH)
    c_q = pltpu.make_async_copy(q_hbm, qall.at[0, 0], loc_sem.at[2])
    c_q.start()
    for dt in (4, 3, 5, 2, 6, 1, 7):
        pl.semaphore_signal(
            barrier, inc=1, device_id={"pool": pool, "tp": (t + dt) % NT}, device_id_type=MESH
        )
    for dx in (2, 1, 3):
        pl.semaphore_signal(barrier, inc=1, device_id=at(0, dx), device_id_type=MESH)
    c_tab = pltpu.make_async_copy(tab_hbm, tab, loc_sem.at[0])
    c_len = pltpu.make_async_copy(len_hbm, lens, loc_sem.at[1])
    c_k = pltpu.make_async_copy(k_hbm.at[0], keys, loc_sem.at[3])
    c_v = pltpu.make_async_copy(v_hbm.at[0], vals, loc_sem.at[4])
    c_w = pltpu.make_async_copy(w_hbm, wall.at[t], loc_sem.at[5])
    c_tab.start()
    c_len.start()
    c_k.start()
    c_v.start()
    c_w.start()
    c_q.wait()
    pl.semaphore_wait(barrier, len(NEAR) + NX - 1 + NT - 1)

    place = {dz: k for k, dz in enumerate(ZORDER)}
    for dz in NEAR:
        k = place[NZ - dz]
        remote(qall.at[0, 0], qall.at[0, k], sq, rq.at[int(k >= DOWN[0])], at(dz, 0))

    sibling = {"pool": pool, "tp": t + 1 - 2 * (t % 2)}
    for dt in (2, 6, 4):
        remote(w_hbm, wall.at[t], sw.at[0], rw.at[0], {"pool": pool, "tp": (t + dt) % NT})
    remote(w_hbm, wall.at[t], sw.at[1], rw.at[1], sibling)

    c_tab.wait()
    c_len.wait()
    tab_t = tab[...].astype(F32)
    len_row = lens[...].astype(F32)
    sub = lax.broadcasted_iota(jnp.int32, (ROWS, ROWS), 0)
    lane = lax.broadcasted_iota(jnp.int32, (ROWS, ROWS), 1)
    sid = (pool * SLOTS + sub // GROUP).astype(F32)
    left = jnp.zeros((ROWS, ROWS), F32)
    sub4 = lax.broadcasted_iota(jnp.int32, (NX * SLOTS, ROWS), 0)
    sid4 = ((z * NX + (x + sub4 // SLOTS) % NX) * SLOTS + sub4 % SLOTS).astype(F32)
    held = jnp.zeros((NX * SLOTS, ROWS), F32)
    for b in range(MAXB):
        entry = tab_t[b : b + 1, :]
        left = jnp.where(entry == sid, len_row - float(BLK * b), left)
        held = jnp.where(entry == sid4, 1.0, held)
    hold[...] = held
    lims[...] = jnp.broadcast_to(jnp.sum(left, axis=1, keepdims=True), (ROWS, ROWS))
    row_of = jnp.sum(
        jnp.where(left > 0.0, (lane + 1).astype(F32), 0.0), axis=1, keepdims=True
    )
    key_col = (row_of - 1.0) * float(GROUP) + (sub[:, 0:1] % GROUP).astype(F32)
    j = lax.broadcasted_iota(jnp.int32, (1, ROWS * GROUP), 1)
    piece = j // (2 * GROUP)
    k_j = piece % NZ
    dz_j = jnp.zeros_like(j)
    for k, dz in enumerate(ZORDER):
        dz_j = jnp.where(k_j == k, dz, dz_j)
    p_j = ((z + dz_j) % NZ) * NX + (x + piece // NZ) % NX
    key_row = ((2 * p_j + j % 2) * GROUP + (j % (2 * GROUP)) // 2).astype(F32)
    for c in range(8):
        cut = slice(c * 128, (c + 1) * 128)
        sel[:, cut] = jnp.where(key_col == key_row[:, cut], 1.0, 0.0).astype(BF16)

    def pieces(cut):
        return pl.ds(cut[0], cut[1] - cut[0])

    def across(cut):
        for dx in (2, 1, 3):
            remote(
                qall.at[0, pieces(cut)],
                qall.at[(NX - dx) % NX, pieces(cut)],
                sqx,
                rqx.at[(NX - dx) % NX],
                at(0, dx),
            )

    arrived(qall.at[0, pieces(DOWN)], rq.at[1])
    remote(qall.at[0, pieces(DOWN)], qall.at[0, pieces(FAR_DOWN)], sq, rq.at[3], at(HUB, 0))
    arrived(qall.at[0, pieces(UP)], rq.at[0])
    count = pl.ds(UP[0], FAR_UP[1] - FAR_UP[0])
    remote(qall.at[0, count], qall.at[0, pieces(FAR_UP)], sq, rq.at[2], at(NZ - HUB, 0))
    across((0, DOWN[1]))
    arrived(qall.at[0, pieces(FAR_UP)], rq.at[2])
    across(FAR_UP)
    arrived(qall.at[0, pieces(FAR_DOWN)], rq.at[3])
    across(FAR_DOWN)
    c_k.wait()
    for s in range(SLOTS):
        keys_t[s] = keys[s].T
    picked = jnp.zeros((ROWS, HD), F32)
    for e in (0, 3, 1, 2):
        if e:
            arrived(qall.at[e], rqx.at[e])
        cut = slice(e * NZ * 2 * GROUP, (e + 1) * NZ * 2 * GROUP)
        picked = picked + dot(sel[:, cut], qall[e].reshape(NZ * 2 * GROUP, HD))
    for dt in (4, 3, 5, 2, 6, 1, 7):
        pl.semaphore_signal(
            seen, inc=1, device_id={"pool": pool, "tp": (t + dt) % NT}, device_id_type=MESH
        )

    scaling = 1.0 / math.sqrt(HD)
    for s in range(SLOTS):
        cut = slice(GROUP * s, GROUP * (s + 1))
        score[cut] = dot(picked[cut].astype(BF16), keys_t[s])
    each = 4
    place_in = lax.broadcasted_iota(jnp.int32, (each * GROUP, BLK), 1).astype(F32)
    inverse = []
    spot = sub % GROUP * SLOTS + sub // GROUP
    levels = jnp.zeros((1, ROWS), F32)
    for c in range(SLOTS // each):
        cut = slice(each * GROUP * c, each * GROUP * (c + 1))
        usable = place_in < lims[cut, 0:1]
        scores = jnp.where(usable, score[cut] * scaling, FLOOR)
        peak = jnp.max(scores, axis=1, keepdims=True)
        weights = jnp.where(usable, jnp.exp(scores - peak), 0.0)
        total = jnp.sum(weights, axis=1, keepdims=True)
        used = total > 0.0
        inverse.append(jnp.where(used, 1.0 / jnp.where(used, total, 1.0), 0.0))
        level = jnp.where(used, peak + jnp.log(jnp.where(used, total, 1.0)), FLOOR)
        levels = levels + jnp.sum(
            jnp.where(lane[cut] == spot[cut], level, 0.0), axis=0, keepdims=True
        )
        for i in range(each):
            s = each * c + i
            sl = slice(GROUP * i, GROUP * (i + 1))
            prob[s] = weights[sl].astype(BF16)
    mine_x = rows_of(x, PAIR * SLOTS)
    st_send[...] = levels
    for dx in (2, 1, 3):
        remote(st_send, st_x.at[(NX - dx) % NX], sst, rst, at(0, dx))
    st_x[0] = st_send[...]
    c_v.wait()
    for s in range(SLOTS):
        sl = slice(GROUP * (s % each), GROUP * (s % each + 1))
        o_f[pl.ds(s, GROUP, stride=SLOTS), :] = dot(prob[s], vals[s]) * inverse[s // each][sl]
    o_send[...] = o_f[...].astype(BF16)
    for dx in (2, 1, 3):
        rows = rows_of((x + dx) % NX, PAIR * SLOTS)
        remote(o_send.at[rows], o_x.at[(NX - dx) % NX], so, ro, at(0, dx))
    o_x[0] = o_send[mine_x, :]

    arrived(st_x.at[pl.ds(1, NX - 1)], rst)
    every = jnp.concatenate(
        [jnp.broadcast_to(st_x[e], (SLOTS, ROWS)) for e in range(NX)], axis=0
    )
    lane4 = lax.broadcasted_iota(jnp.int32, (NX * SLOTS, ROWS), 1)
    ws = []
    is_held = hold[...] > 0.0
    for hh in range(PAIR):
        mine = lane4 == (x * PAIR + hh) * SLOTS + sub4 % SLOTS
        level = jnp.sum(jnp.where(mine, every, 0.0), axis=1, keepdims=True)
        top = jnp.max(jnp.where(is_held, level, FLOOR), axis=0, keepdims=True)
        w = jnp.where(is_held, jnp.exp(level - top), 0.0)
        total = jnp.sum(w, axis=0, keepdims=True)
        used = total > 0.0
        total = jnp.where(used, total, 1.0)
        w = w / total
        coarse = w.astype(BF16)
        ws.append((coarse, (w - coarse.astype(F32)).astype(BF16)))
        zst_send[hh : hh + 1, :] = jnp.where(used, top + jnp.log(total), FLOOR)
    pl.semaphore_wait(seen, NT - 1)

    def hand(dz, source, target, send, recv):
        to = at(dz, 0)
        to["tp"] = finisher(dz)
        if dz:
            remote(source, target, send, recv, to)
            return

        @pl.when(finisher(0) != t)
        def _():
            remote(source, target, send, recv, to)

        @pl.when(finisher(0) == t)
        def _():
            pltpu.make_async_copy(source, target, recv).start()

    def left_here(ref, send):
        @pl.when(finisher(0) != t)
        def _():
            arrived(ref, send)

    for dz in FAR_FIRST + (0,):
        hand(dz, zst_send, zst.at[(NZ - dz) % NZ], szs, rzs)

    arrived(o_x.at[pl.ds(1, NX - 1)], ro)
    for hh in range(PAIR):
        data = jnp.concatenate(
            [o_x[e, hh * SLOTS : (hh + 1) * SLOTS, :] for e in range(NX)], axis=0
        )
        both = dot(ws[hh][0], data, ((0,), (0,))) + dot(ws[hh][1], data, ((0,), (0,)))
        part[:, hh * HD : (hh + 1) * HD] = both.astype(BF16)
    for dz in FAR_FIRST + (0,):
        hand(dz, part.at[rows_of(finisher(dz), BAND)], rs.at[(NZ - dz) % NZ], srs, rrs)
    my_band = rows_of(t, BAND)

    arrived(wall.at[pl.ds(0, 3)], rw.at[0])
    for dt in (2, 6, 4):
        origin = (t + dt) % NT
        remote(wall.at[origin], wall.at[origin], sw.at[1], rw.at[1], sibling)

    arrived(qall.at[0, pl.ds(0, NZ - 1)], sq)
    arrived(qall.at[pl.ds(0, NX - 1)], sqx)
    arrived(wall.at[pl.ds(0, 3)], sw.at[0])
    arrived(st_x.at[pl.ds(0, NX - 1)], sst)
    arrived(o_x.at[pl.ds(0, NX - 1)], so)
    arrived(zst.at[pl.ds(0, NZ - 1)], szs)
    left_here(zst.at[0], szs)

    arrived(zst, rzs)
    scales = []
    for hh in range(PAIR):
        level = jnp.concatenate([zst[e, hh : hh + 1, :] for e in range(NZ)], axis=0)
        w = jnp.exp(level - jnp.max(level, axis=0, keepdims=True))
        scales.append(w / jnp.sum(w, axis=0, keepdims=True))
    pad = jnp.zeros((ROWS - PAIR * NZ, ROWS), F32)
    scale_t[...] = jnp.transpose(jnp.concatenate(scales + [pad], axis=0))
    cols = scale_t[my_band, :]
    for e in range(NZ):
        for hh in range(PAIR):
            zw[e, :, hh * HD : (hh + 1) * HD] = jnp.broadcast_to(
                cols[:, hh * NZ + e : hh * NZ + e + 1], (BAND, HD)
            )
    arrived(rs, rrs)
    acc = jnp.zeros((BAND, PAIR * HD), F32)
    for e in range(NZ):
        acc = acc + rs[e].astype(F32) * zw[e]
    band[...] = acc.astype(BF16)

    reach = NZ // 2
    lowest = (z - 4 + t % 2 + NZ) % NZ
    skip = (NZ - lowest) * (lowest // (reach + 1))

    def end(step, dx):
        zz = (lowest + (step + skip) % reach) % NZ
        return zz, pltpu.make_async_remote_copy(
            src_ref=band,
            dst_ref=fin.at[(NX - dx) % NX, theirs],
            send_sem=sfin,
            recv_sem=rfin.at[(NX - dx) % NX],
            device_id={"pool": zz * NX + (x + dx) % NX, "tp": t},
            device_id_type=MESH,
        )

    for step in range(reach):
        for dx in (2, 1, 3, 0):
            zz, copy = end(step, dx)
            if dx:
                copy.start()
                continue

            @pl.when(zz != z)
            def _(copy=copy):
                copy.start()

    pltpu.make_async_copy(band, fin.at[0, theirs], rfin.at[0]).start()
    arrived(rs.at[pl.ds(0, NZ - 1)], srs)
    left_here(rs.at[0], srs)

    c_w.wait()
    arrived(wall.at[pl.ds(0, NX)], rw.at[1])
    arrived(wall.at[pl.ds(0, NX)], sw.at[1])
    acc = jnp.zeros((BAND, HD), F32)
    for e in (0, 1, 3, 2):
        arrived(fin.at[e], rfin.at[e])
        rows = rows_of((x + e) % NX, PAIR * HD)
        for n in range(NT):
            acc = acc + dot(fin[e, n], wall[n, rows, :])
    out_ref[...] = acc.astype(BF16)
    arrived(fin.at[pl.ds(0, NX - 1)], sfin)
    arrived(fin.at[0, pl.ds(0, NT - 1)], sfin)


def on_device(queries, key_cache, value_cache, out_weight, lengths, block_table):
    q = queries.reshape(2, GROUP, HD).transpose(1, 0, 2).reshape(2 * GROUP, HD)
    hbm = pl.BlockSpec(memory_space=pltpu.HBM)
    dma = pltpu.SemaphoreType.DMA
    vmem = pltpu.VMEM
    return pl.pallas_call(
        kernel,
        out_shape=pltpu.VMEM((BAND, HD), BF16),
        in_specs=[hbm] * 6,
        out_specs=pl.BlockSpec(memory_space=pltpu.VMEM),
        scratch_shapes=[
            vmem((MAXB, ROWS), jnp.int32),
            vmem((1, ROWS), jnp.int32),
            vmem((SLOTS, BLK, HD), BF16),
            vmem((SLOTS, HD, BLK), BF16),
            vmem((SLOTS, BLK, HD), BF16),
            vmem((NX, NZ, 2 * GROUP, HD), BF16),
            vmem((ROWS, ROWS * GROUP), BF16),
            vmem((ROWS, ROWS), F32),
            vmem((NX * SLOTS, ROWS), F32),
            vmem((ROWS, BLK), F32),
            vmem((SLOTS, GROUP, BLK), BF16),
            vmem((ROWS, HD), F32),
            vmem((ROWS, HD), BF16),
            vmem((1, ROWS), F32),
            vmem((NX, 1, ROWS), F32),
            vmem((NX, PAIR * SLOTS, HD), BF16),
            vmem((PAIR, ROWS), F32),
            vmem((NZ, PAIR, ROWS), F32),
            vmem((ROWS, ROWS), F32),
            vmem((NZ, BAND, PAIR * HD), F32),
            vmem((ROWS, PAIR * HD), BF16),
            vmem((NZ, BAND, PAIR * HD), BF16),
            vmem((BAND, PAIR * HD), BF16),
            vmem((NX, NT, BAND, PAIR * HD), BF16),
            vmem((NT, GROUP * HD, HD), BF16),
            dma((6,)),
            dma,
            dma((4,)),
            dma,
            dma((NX,)),
            dma((2,)),
            dma((2,)),
            dma,
            dma,
            dma,
            dma,
            dma,
            dma,
            dma,
            dma,
            dma,
            dma((NX,)),
            pltpu.SemaphoreType.REGULAR,
        ],
        compiler_params=pltpu.CompilerParams(
            collective_id=0, has_side_effects=True, vmem_limit_bytes=56 * 1024 * 1024
        ),
        cost_estimate=pl.CostEstimate(
            flops=400_000_000, bytes_accessed=5_000_000, transcendentals=70_000
        ),
        name="lent_attention",
    )(q, key_cache, value_cache, out_weight, lengths.reshape(1, ROWS), block_table.T)


def solution(mesh):
    return jax.shard_map(
        on_device,
        mesh=mesh,
        in_specs=(
            P("pool", "tp"),
            P("tp", "pool", None, None),
            P("tp", "pool", None, None),
            P("tp", "pool"),
            P(),
            P(),
        ),
        out_specs=P("tp", "pool"),
        check_vma=False,
    )
```
